256 devices in a mesh: dp: 8 (over x, core), seq: 32 (over z, y).
Axes of the slice: x: 4, y: 4, z: 8, core: 2. Of those that a mesh axis runs over, the one named last changes fastest.
Arguments:
- queries: bfloat16 [49152, 512], P(('dp', 'seq')), may hold values from -6 to 6
- key_vectors: bfloat16 [49152, 512], P(('dp', 'seq')), may hold values from -6 to 6
- value_vectors: bfloat16 [49152, 512], P(('dp', 'seq')), may hold values from -6 to 6
- gate_values: bfloat16 [49152, 512], P(('dp', 'seq')), may hold values from -6 to 6
- norm_gain: float32 [512], replicated, may hold values from 0.5 to 2
- out_weight: bfloat16 [512, 1024], replicated, may hold values from -0.25 to 0.25
- out_grad: bfloat16 [49152, 1024], P(('dp', 'seq')), may hold values from -6 to 6
- history_lengths: int32 [8, 4], P('dp'), may hold values from 1 to 6048, 6144 in all within a row
Outputs:
- layer_out: bfloat16 [49152, 1024], P(('dp', 'seq'))
- query_grad: bfloat16 [49152, 512], P(('dp', 'seq'))
- key_grad: bfloat16 [49152, 512], P(('dp', 'seq'))
- value_grad: bfloat16 [49152, 512], P(('dp', 'seq'))
- gate_grad: bfloat16 [49152, 512], P(('dp', 'seq'))
- weight_grad: float32 [512, 1024], P('seq')
The draws below stay inside these ranges and needn't reach their ends.
Inputs may be any that keep to these rules, and one draw needn't show every extreme that they name: `history_lengths`: in every row the 4 lengths sum to 6144, and the largest of them is exactly 6048.
All inputs are finite; a program needn't handle non-finite values.
Results may differ from the reference program's by a relative error of at most 0.015.
Values may be sent and summed in bfloat16 or wider, within the bound.
A program may use at most 128 MiB of HBM per device.

```python
import math
import jax
import jax.numpy as jnp
import numpy as np
from jax import lax

D = 1024
HEADS = 4
HEAD = 128
HISTS = 4
TOK_DEV = 192
QK = 512
SEQ_TOK = 6144
ALL_TOK = 49152
N_DP = 8


def block_levels(own_key, shape, pieces, least, top_value):
    factor_of, own = 1.0, jax.random.fold_in(own_key, 6)
    for axis_at, shards_of in pieces:
        draws = jnp.exp(jax.random.uniform(jax.random.fold_in(own, axis_at), (shards_of,), jnp.float32, least / len(pieces), top_value / len(pieces)))
        factor_of = factor_of * jnp.repeat(draws, shape[axis_at] // shards_of).reshape([-1 if axis == axis_at else 1 for axis in range(len(shape))])
    return factor_of


def length_profile(number_of, total, most, lean):
    portions = [(1 << 20) // math.isqrt(grade ** lean) + 1 for grade in range(2, number_of + 1)]
    surplus, given = total - most - (number_of - 1), [1] * (number_of - 1)
    while surplus > 0:
        free = [i for i in range(number_of - 1) if given[i] < most]
        whole, left = sum([portions[i] for i in free]), surplus
        for i in free:
            more = min(most - given[i], max(1, left * portions[i] // whole), surplus)
            given[i] = given[i] + more
            surplus = surplus - more
    return np.array([most] + given)


def ragged_sizes(key, count, total, limit, skew):
    if count == 2:
        one = jax.random.randint(key, (), max(1, total - limit), min(limit, total - 1) + 1)
        return jnp.stack([one, total - one])
    tallies = jnp.asarray(length_profile(count, total, limit, skew), jnp.int32)
    twos = (count - 1) // 2
    giver, sink = tallies[1:1 + 2 * twos:2], tallies[2:2 + 2 * twos:2]
    slack = jnp.minimum(giver - 1, limit - sink)
    shifted = jax.random.randint(jax.random.fold_in(key, 1), (twos,), 0, 1 << 20) % (slack + 1)
    tallies = tallies.at[1:1 + 2 * twos:2].set(giver - shifted).at[2:2 + 2 * twos:2].set(sink + shifted)
    return tallies[jax.random.permutation(jax.random.fold_in(key, 2), count)]


def scatter_about(stream_key, extent, spread, most, shards=(), kind=jnp.bfloat16):
    factor_of = block_levels(stream_key, extent, shards, -0.22, 0.18) if shards else 1.0
    entries = jax.random.normal(stream_key, extent, jnp.float32) * spread * factor_of
    return jnp.minimum(jnp.maximum(entries, -most), most).astype(kind)


def setup_inputs(seed: int = 0) -> dict:
    seeds = jax.random.split(jax.random.key(seed), 9)
    queries = scatter_about(seeds[0], (ALL_TOK, QK), 1.0, 6.0, ((0, 256),))
    key_vectors = scatter_about(seeds[1], (ALL_TOK, QK), 1.0, 6.0, ((0, 256),))
    value_vectors = scatter_about(seeds[2], (ALL_TOK, QK), 1.0, 6.0, ((0, 256),))
    gate_values = scatter_about(seeds[3], (ALL_TOK, QK), 1.0, 6.0, ((0, 256),))
    norm_gain = jnp.clip(jnp.exp(jax.random.uniform(seeds[4], (QK,), jnp.float32, math.log(0.5), math.log(2.0))), 0.5, 2.0)
    out_weight = scatter_about(seeds[5], (QK, D), QK ** -0.5, 0.25)
    out_grad = scatter_about(seeds[6], (ALL_TOK, D), 1.0, 6.0, ((0, 256),))
    history_lengths = jax.vmap(lambda own: ragged_sizes(own, HISTS, SEQ_TOK, SEQ_TOK - TOK_DEV // 2, 2))(jax.random.split(seeds[7], N_DP)).reshape((N_DP, HISTS)).astype(jnp.int32)
    return dict(queries=queries, key_vectors=key_vectors, value_vectors=value_vectors, gate_values=gate_values, norm_gain=norm_gain, out_weight=out_weight, out_grad=out_grad, history_lengths=history_lengths)


NORM_EPSILON = 1e-05

def rounded(values):
    return lax.optimization_barrier(values.astype(jnp.bfloat16)).astype(jnp.float32)

def history_of(history_ends, places):
    return lax.optimization_barrier(jnp.sum((places[:, None] >= history_ends[None, :]).astype(jnp.int32), axis=1))

def history_row(items, norm_gain, out_weight):
    queries, key_vectors, value_vectors, gate_values, out_grad, history_lengths = items
    history_span = queries.shape[0]
    query_block = min(512, history_span)
    block_count = history_span // query_block
    score_scale = HEAD ** (-0.5)
    places = jnp.arange(history_span, dtype=jnp.int32)
    history_ends = jnp.cumsum(history_lengths).astype(jnp.int32)
    owners = history_of(history_ends, places)
    key_heads = key_vectors.astype(jnp.float32).reshape(history_span, HEADS, HEAD)
    value_heads = value_vectors.astype(jnp.float32).reshape(history_span, HEADS, HEAD)
    block_ids = jnp.arange(block_count, dtype=jnp.int32)

    def scored(block_index):
        start_row = (block_index * query_block).astype(jnp.int32)
        query_heads = lax.dynamic_slice_in_dim(queries, start_row, query_block, 0)
        query_heads = query_heads.astype(jnp.float32).reshape(query_block, HEADS, HEAD)
        query_places = start_row + jnp.arange(query_block, dtype=jnp.int32)
        same_owner = history_of(history_ends, query_places)[:, None] == owners[None, :]
        visible = (same_owner & (query_places[:, None] >= places[None, :])).astype(jnp.float32)
        scores = jnp.einsum('qhd,khd->hqk', query_heads, key_heads) * score_scale
        gates = jax.nn.sigmoid(scores)
        return (query_heads, start_row, visible, scores, gates)

    def forward_block(block_index):
        query_heads, start_row, visible, scores, gates = scored(block_index)
        weights = rounded(scores * gates * visible)
        attention = jnp.einsum('hqk,khd->qhd', weights, value_heads)
        return attention.reshape(query_block, HEADS * HEAD)
    attention = lax.map(forward_block, block_ids).reshape(history_span, HEADS * HEAD)
    row_mean = lax.optimization_barrier(jnp.mean(attention, axis=1, keepdims=True))
    centred = attention - row_mean
    inv_std = 1.0 / jnp.sqrt(lax.optimization_barrier(jnp.mean(centred * centred, axis=1, keepdims=True)) + NORM_EPSILON)
    unit_attn = centred * inv_std
    gain_values = norm_gain.astype(jnp.float32)
    normed = unit_attn * gain_values
    gated_out = (normed * gate_values.astype(jnp.float32)).astype(jnp.bfloat16)
    layer_out = jnp.dot(gated_out, out_weight, preferred_element_type=jnp.float32).astype(jnp.bfloat16)
    grad_gated = jnp.dot(out_grad, out_weight.T, preferred_element_type=jnp.float32)
    gate_grad = (grad_gated * normed).astype(jnp.bfloat16)
    grad_hat = grad_gated * gate_values.astype(jnp.float32) * gain_values
    grad_mean = lax.optimization_barrier(jnp.mean(grad_hat, axis=1, keepdims=True))
    grad_proj = lax.optimization_barrier(jnp.mean(grad_hat * unit_attn, axis=1, keepdims=True))
    attn_grad = rounded(inv_std * (grad_hat - grad_mean - unit_attn * grad_proj))
    grad_heads = attn_grad.reshape(history_span, HEADS, HEAD)

    def backward_block(carried, block_index):
        key_total, value_total = carried
        query_heads, start_row, visible, scores, gates = scored(block_index)
        weights = rounded(scores * gates * visible)
        block_grads = lax.dynamic_slice_in_dim(grad_heads, start_row, query_block, 0)
        grad_weights = jnp.einsum('qhd,khd->hqk', block_grads, value_heads)
        grad_scores = rounded(grad_weights * gates * (1.0 + scores * (1.0 - gates)) * visible)
        query_part = jnp.einsum('hqk,khd->qhd', grad_scores, key_heads) * score_scale
        key_total = key_total + jnp.einsum('hqk,qhd->khd', grad_scores, query_heads) * score_scale
        value_total = value_total + jnp.einsum('hqk,qhd->khd', weights, block_grads)
        return ((key_total, value_total), query_part.reshape(query_block, HEADS * HEAD))
    zero_heads = jnp.zeros((history_span, HEADS, HEAD), jnp.float32)
    (key_total, value_total), query_parts = lax.scan(backward_block, (zero_heads, zero_heads), block_ids)
    query_grad = query_parts.reshape(history_span, HEADS * HEAD).astype(jnp.bfloat16)
    key_grad = key_total.reshape(history_span, HEADS * HEAD).astype(jnp.bfloat16)
    value_grad = value_total.reshape(history_span, HEADS * HEAD).astype(jnp.bfloat16)
    return (layer_out, query_grad, key_grad, value_grad, gate_grad, gated_out)

def reference(queries, key_vectors, value_vectors, gate_values, norm_gain, out_weight, out_grad, history_lengths):

    def by_row(array):
        return array.reshape(N_DP, SEQ_TOK, array.shape[1])

    def one_row(items):
        return history_row(items, norm_gain, out_weight)
    results = lax.map(one_row, (by_row(queries), by_row(key_vectors), by_row(value_vectors), by_row(gate_values), by_row(out_grad), history_lengths))
    flat = [stacked.reshape(ALL_TOK, stacked.shape[2]) for stacked in results]
    weight_grad = jnp.dot(flat[5].T, out_grad, preferred_element_type=jnp.float32) * ALL_TOK ** (-0.5)
    return (flat[0], flat[1], flat[2], flat[3], flat[4], weight_grad)
```

```python
import jax
import jax.numpy as jnp
from jax import lax
from jax.experimental import pallas as pl
from jax.experimental.pallas import tpu as pltpu
from jax.sharding import PartitionSpec as P

TOK = 192
HEAD = 128
HEADS = 4
QK = HEAD * HEADS
WIDTH = 1024
SLOTS = 4
YN = 4
ZN = 8
CHUNK = YN * TOK
SCALE = HEAD ** (-0.5)
EPS = 1e-5
ALL_ROWS = 49152
BF = jnp.bfloat16
F32 = jnp.float32
MESH = pl.DeviceIdType.MESH
NT = (((1,), (1,)), ((), ()))
NN = (((1,), (0,)), ((), ()))


def dot(a, b, dims=NN):
    return lax.dot_general(a, b, dims, preferred_element_type=F32)


def layer_kernel(
    q_ref, k_ref, v_ref, u_ref, og_ref, w_ref, gain_ref, gain_heads_ref, ends_ref,
    lay_ref, dq_ref, dk_ref, dv_ref, gg_out_ref, wg_ref,
    k_all, v_all, q_blk, gh_blk, gh_own, gg, ends_sib, att, stat,
    nrm_blk, do_blk, nrm_in, dq_acc, dq_blk,
    part_out, part_in, part_own, red, ring_in, ring_acc, fin,
    w_part, w_sib, w_sum, w_x, w_64, w_y, w_16, w_z,
    a_send, a_recv, y_send, y_recv, s_send, s_recv, e_sem, t_send, t_recv, n_send, n_recv,
    p_send, p_recv, r_send, r_recv, f_send, f_recv,
    ws_sem, wx_send, wx_recv, wy_send, wy_recv, wz_send, wz_recv, wb_send, wb_recv,
):
    d = lax.axis_index("dp")
    s = lax.axis_index("seq")
    x, c = d // 2, d % 2
    z, y = s // YN, s % YN
    row, head = z // HEADS, z % HEADS
    core_of_z = ((z + 1) // 2) % 2
    slot_of_z = z // 2
    right, left, across = (y + 1) % YN, (y + 3) % YN, (y + 2) % YN

    def zmap(core, j):
        return 2 * j + core if j % 2 == 0 else 2 * j + 1 - core

    def at(core, zz, yy):
        return (2 * x + core, YN * zz + yy)

    sibling = at(1 - c, z, y)
    to_right, to_left = at(c, z, right), at(c, z, left)

    def remote(src, dst, send, recv, device):
        return pltpu.make_async_remote_copy(
            src_ref=src, dst_ref=dst, send_sem=send, recv_sem=recv,
            device_id=device, device_id_type=MESH,
        )

    def landed(dst, sem):
        pltpu.make_async_copy(dst, dst, sem).wait()

    home = [(at(core_of_z, HEADS * c + h, y), (core_of_z == c) & (HEADS * c + h == z)) for h in range(HEADS)]
    owner = [(at(row, zmap(c, j), y), (row == c) & (zmap(c, j) == z)) for j in range(SLOTS)]
    own_z = [zmap(c, j) for j in range(SLOTS)]
    sib_z = [zmap(1 - c, j) for j in range(SLOTS)]

    bar = pltpu.get_barrier_semaphore()

    def greet(device):
        pl.semaphore_signal(bar, inc=1, device_id=device, device_id_type=MESH)

    for device, mine in home + owner:
        @pl.when(jnp.logical_not(mine))
        def _():
            greet(device)
    for step in range(1, YN):
        greet(at(c, z, (y + step) % YN))
        greet((2 * ((x + step) % 4) + c, s))
    greet(sibling)
    for h in range(HEADS):
        @pl.when(h != head)
        def _():
            greet(at(c, HEADS * row + h, y))
    collector = z == d

    @pl.when(collector)
    def _():
        for zz in range(ZN):
            @pl.when(zz != z)
            def _():
                greet((d, YN * zz + y))

    @pl.when(jnp.logical_not(collector))
    def _():
        greet((z, s))

    selfs = (home[0][1] | home[1][1] | home[2][1] | home[3][1]).astype(jnp.int32)
    pl.semaphore_wait(bar, 8 - 2 * selfs + 3 + 3 + 1 + 3 + jnp.where(collector, ZN - 1, 1))

    block = YN * z + y

    def scatter(a, src, dst):
        for h in range(HEADS):
            device, mine = home[h]
            cols = src.at[:, h * HEAD:(h + 1) * HEAD]

            @pl.when(mine)
            def _():
                pltpu.make_async_copy(cols, dst, a_recv.at[a, slot_of_z]).start()

            @pl.when(jnp.logical_not(mine))
            def _():
                remote(cols, dst, a_send.at[a, h], a_recv.at[a, slot_of_z], device).start()

    remote(ends_ref, ends_sib, e_sem.at[0], e_sem.at[1], sibling).start()
    scatter(0, k_ref, k_all.at[block])
    scatter(1, v_ref, v_all.at[block])
    scatter(2, q_ref, q_blk.at[slot_of_z])
    gg[...] = dot(og_ref[...], w_ref[...], NT)
    gh_own[...] = (gg[...] * u_ref[...].astype(F32) * gain_ref[...]).astype(BF)
    scatter(3, gh_own, gh_blk.at[slot_of_z])

    kv = (k_all, v_all)
    for j in range(SLOTS):
        for a in range(2):
            ref = kv[a].at[YN * own_z[j] + y]
            landed(ref, a_recv.at[a, j])
            remote(ref, ref, y_send.at[a, j, 0], y_recv.at[a, j, 0], to_right).start()
            remote(ref, ref, y_send.at[a, j, 1], y_recv.at[a, j, 1], to_left).start()
    for j in range(SLOTS):
        ref = k_all.at[YN * own_z[j] + left]
        landed(ref, y_recv.at[0, j, 0])
        remote(ref, ref, y_send.at[0, j, 2], y_recv.at[0, j, 2], to_right).start()
        ref = v_all.at[YN * own_z[j] + right]
        landed(ref, y_recv.at[1, j, 1])
        remote(ref, ref, y_send.at[1, j, 2], y_recv.at[1, j, 2], to_left).start()

    landed(ends_sib, e_sem.at[1])
    ends = jnp.where(row == c, ends_ref[...], ends_sib[...])

    def start_of(place, e0, e1, e2):
        return jnp.where(place >= e2, e2, jnp.where(place >= e1, e1, jnp.where(place >= e0, e0, 0)))

    for j in range(SLOTS):
        landed(q_blk.at[j], a_recv.at[2, j])
    att[...] = jnp.zeros_like(att)

    def attend(j, zq, zk):
        place = (YN * zq + y) * TOK + lax.broadcasted_iota(jnp.int32, (TOK, 1), 0)
        begin = start_of(place, ends[0:1, 0:1], ends[1:2, 0:1], ends[2:3, 0:1])
        keys = k_all[pl.ds(YN * zk, YN)].reshape(CHUNK, HEAD)
        values = v_all[pl.ds(YN * zk, YN)].reshape(CHUNK, HEAD)
        half = dot(q_blk[j], keys, NT) * (0.5 * SCALE)
        key_place = zk * CHUNK + lax.broadcasted_iota(jnp.int32, (TOK, CHUNK), 1)
        visible = (key_place <= place) & (key_place >= begin)
        weights = jnp.where(visible, half * (1.0 + jnp.tanh(half)), 0.0).astype(BF)
        att[j] += dot(weights, values)

    def zmap_at(core, j):
        return 2 * j + jnp.where(j % 2 == 0, core, 1 - core)

    def forward(zk, first):
        def step(j, carry):
            attend(j, zmap_at(c, j), zk)
            return carry
        lax.fori_loop(first, SLOTS, step, 0)

    for j in range(SLOTS):
        for a in range(2):
            for n, yy in ((0, left), (1, right), (2, across)):
                if (a, n) in ((0, 0), (1, 1)):
                    continue
                landed(kv[a].at[YN * own_z[j] + yy], y_recv.at[a, j, n])
            ref = kv[a].at[pl.ds(YN * own_z[j], YN)]
            remote(ref, ref, s_send.at[a, j], s_recv.at[a, j], sibling).start()
        forward(own_z[j], j)
    for j in range(SLOTS):
        for a in range(2):
            landed(kv[a].at[pl.ds(YN * sib_z[j], YN)], s_recv.at[a, j])
        forward(sib_z[j], j + (own_z[j] < sib_z[j]).astype(jnp.int32))

    for j in range(SLOTS):
        landed(gh_blk.at[j], a_recv.at[3, j])
    flat_att = att[...].reshape(SLOTS * TOK, HEAD)
    flat_gh = gh_blk[...].reshape(SLOTS * TOK, HEAD).astype(F32)
    head_mean = jnp.mean(flat_att, axis=1, keepdims=True)
    centred = flat_att - head_mean
    lane = lax.broadcasted_iota(jnp.int32, (SLOTS * TOK, HEAD), 1)
    packed = jnp.where(lane == 0, head_mean, 0.0)
    packed = jnp.where(lane == 1, jnp.sum(centred * centred, axis=1, keepdims=True), packed)
    packed = jnp.where(lane == 2, jnp.sum(flat_gh * centred, axis=1, keepdims=True), packed)
    packed = jnp.where(lane == 3, jnp.sum(flat_gh, axis=1, keepdims=True), packed)
    stat[head] = jnp.transpose(packed)[0:8]
    for h in range(HEADS):
        @pl.when(h != head)
        def _():
            remote(stat.at[head], stat.at[head], t_send.at[h], t_recv.at[head],
                   at(c, HEADS * row + h, y)).start()
    for h in range(HEADS):
        @pl.when(h != head)
        def _():
            landed(stat.at[h], t_recv.at[h])
    means = [stat[h, 0:1, :] for h in range(HEADS)]
    grads = [stat[h, 3:4, :] for h in range(HEADS)]
    mean = (means[0] + means[1] + means[2] + means[3]) * (1.0 / HEADS)
    square, cross, grad_sum = 0.0, 0.0, 0.0
    for h in range(HEADS):
        off = means[h] - mean
        square += stat[h, 1:2, :] + HEAD * off * off
        cross += stat[h, 2:3, :] + off * grads[h]
        grad_sum += grads[h]
    inv_std = 1.0 / jnp.sqrt(square * (1.0 / QK) + EPS)
    rows = jnp.concatenate(
        [mean, inv_std, grad_sum * (1.0 / QK), cross * inv_std * (1.0 / QK),
         jnp.zeros((HEAD - 4, SLOTS * TOK), F32)], axis=0)
    cols = jnp.transpose(rows)
    mean_c, inv_c, gmean_c, proj_c = (cols[:, i:i + 1] for i in range(4))
    unit = (flat_att - mean_c) * inv_c
    nrm_blk[...] = (unit * gain_heads_ref[head]).astype(BF).reshape(SLOTS, TOK, HEAD)
    do_blk[...] = (inv_c * (flat_gh - gmean_c - unit * proj_c)).astype(BF).reshape(SLOTS, TOK, HEAD)

    head_cols = pl.ds(pl.multiple_of(head * HEAD, HEAD), HEAD)

    def give_back(src, dst, send, recv, j):
        device, mine = owner[j]

        @pl.when(mine)
        def _():
            pltpu.make_async_copy(src, dst, recv).start()

        @pl.when(jnp.logical_not(mine))
        def _():
            remote(src, dst, send, recv, device).start()

    for j in range(SLOTS):
        give_back(nrm_blk.at[j], nrm_in.at[:, head_cols], n_send.at[j], n_recv.at[head], j)

    lanes = lax.broadcasted_iota(jnp.int32, (1, SLOTS * TOK), 1)
    slot_z = jnp.where(lanes < TOK, own_z[0], jnp.where(
        lanes < 2 * TOK, own_z[1], jnp.where(lanes < 3 * TOK, own_z[2], own_z[3])))
    slot_n = jnp.where(lanes < TOK, 0, jnp.where(lanes < 2 * TOK, 1, jnp.where(lanes < 3 * TOK, 2, 3)))
    query_place = (YN * slot_z + y) * TOK + lanes - slot_n * TOK
    query_begin = start_of(query_place, ends[0:1], ends[1:2], ends[2:3])
    dq_acc[...] = jnp.zeros_like(dq_acc)

    def backward(zk, first, store):
        width = (SLOTS - first) * TOK
        lo = first * TOK
        queries = q_blk[first:].reshape(width, HEAD)
        grads_out = do_blk[first:].reshape(width, HEAD)
        place, begin = query_place[:, lo:], query_begin[:, lo:]

        def step(b, carry):
            keys = k_all[YN * zk + b]
            values = v_all[YN * zk + b]
            half = dot(keys, queries, NT) * (0.5 * SCALE)
            gw = dot(values, grads_out, NT)
            t = jnp.tanh(half)
            plus = 1.0 + t
            key_place = (YN * zk + b) * TOK + lax.broadcasted_iota(jnp.int32, (TOK, width), 0)
            visible = (key_place <= place) & (key_place >= begin)
            weights = jnp.where(visible, half * plus, 0.0).astype(BF)
            ds = jnp.where(visible, gw * plus * (1.0 + half * (1.0 - t)), 0.0).astype(BF)
            store(b, dot(ds, queries), dot(weights, grads_out))
            dq_acc[:, lo:] += dot(jnp.transpose(keys), ds)
            return carry

        lax.fori_loop(0, YN, step, 0)

    def backward_sib(j):
        def store(b, dk, dv):
            part_out[0, j, b] = dk.astype(BF)
            part_out[1, j, b] = dv.astype(BF)

        full = own_z[j] > sib_z[j]

        @pl.when(full)
        def _():
            backward(sib_z[j], j, store)

        @pl.when(jnp.logical_not(full))
        def _():
            if j + 1 < SLOTS:
                backward(sib_z[j], j + 1, store)
            else:
                for a in range(2):
                    part_out[a, j] = jnp.zeros((YN, TOK, HEAD), BF)

        for a in range(2):
            remote(part_out.at[a, j], part_in.at[a, j], p_send.at[a, j], p_recv.at[a, j], sibling).start()

    def backward_own(j):
        def store(b, dk, dv):
            part_own[0, b] = dk
            part_own[1, b] = dv

        backward(own_z[j], j, store)

    def chip_sum(j):
        for a in range(2):
            landed(part_in.at[a, j], p_recv.at[a, j])
            red[a, j] = (part_own[a] + part_in[a, j].astype(F32)).astype(BF)
        ring(0, j, red.at[0, j, across], to_right)
        ring(1, j, red.at[1, j, across], to_left)
        ring(2, j, red.at[1, j, right], to_right)
        ring(3, j, red.at[0, j, left], to_left)

    def ring(n, j, src, device):
        remote(src, ring_in.at[n, j], r_send.at[n, j], r_recv.at[n, j], device).start()

    def relay(j):
        landed(ring_in.at[0, j], r_recv.at[0, j])
        ring_acc[0, j] = (red[0, j, right].astype(F32) + ring_in[0, j].astype(F32)).astype(BF)
        ring(4, j, ring_acc.at[0, j], to_right)
        landed(ring_in.at[1, j], r_recv.at[1, j])
        ring_acc[1, j] = (red[1, j, left].astype(F32) + ring_in[1, j].astype(F32)).astype(BF)
        ring(5, j, ring_acc.at[1, j], to_left)

    def finish(j):
        for n in (2, 3, 4, 5):
            landed(ring_in.at[n, j], r_recv.at[n, j])
        fin[0, j] = ((red[0, j, y].astype(F32) + ring_in[3, j].astype(F32) + ring_in[4, j].astype(F32))
                     * (0.5 * SCALE)).astype(BF)
        fin[1, j] = (red[1, j, y].astype(F32) + ring_in[2, j].astype(F32)
                     + ring_in[5, j].astype(F32)).astype(BF)
        give_back(fin.at[0, j], dk_ref.at[:, head_cols], f_send.at[0, j], f_recv.at[0, head], j)
        give_back(fin.at[1, j], dv_ref.at[:, head_cols], f_send.at[1, j], f_recv.at[1, head], j)

    def project():
        for h in range(HEADS):
            landed(nrm_in.at[:, h * HEAD:(h + 1) * HEAD], n_recv.at[h])
        normed = nrm_in[...].astype(F32)
        gated = (normed * u_ref[...].astype(F32)).astype(BF)
        gg_out_ref[...] = (gg[...] * normed).astype(BF)
        w_part[...] = dot(jnp.transpose(gated), og_ref[...]).astype(BF).reshape(4, 2, 64, WIDTH)
        remote(w_part.at[:, 1 - c], w_sib, ws_sem.at[0], ws_sem.at[1], sibling).start()
        lay_ref[...] = dot(gated, w_ref[...]).astype(BF)

    def weight_x():
        landed(w_sib, ws_sem.at[1])
        w_sum[...] = (w_part[:, c].astype(F32) + w_sib[...].astype(F32)).astype(BF)
        for step in range(1, 4):
            to = (x + step) % 4
            remote(w_sum.at[to], w_x.at[step - 1], wx_send.at[step - 1], wx_recv.at[step - 1],
                   (2 * to + c, s)).start()

    def weight_y():
        total = w_sum[x].astype(F32)
        for step in range(3):
            landed(w_x.at[step], wx_recv.at[step])
            total += w_x[step].astype(F32)
        w_64[...] = total.astype(BF).reshape(YN, 16, WIDTH)
        for step in range(1, YN):
            to = (y + step) % YN
            remote(w_64.at[to], w_y.at[step - 1], wy_send.at[step - 1], wy_recv.at[step - 1],
                   at(c, z, to)).start()

    def weight_z():
        total = w_64[y].astype(F32)
        for step in range(3):
            landed(w_y.at[step], wy_recv.at[step])
            total += w_y[step].astype(F32)
        w_16[...] = total.astype(BF)

        @pl.when(jnp.logical_not(collector))
        def _():
            remote(w_16, w_z.at[z], wz_send, wz_recv.at[z], (d, YN * d + y)).start()

    def weight_all():
        @pl.when(collector)
        def _():
            w_z[z] = w_16[...]
            for zz in range(ZN):
                @pl.when(zz != z)
                def _():
                    landed(w_z.at[zz], wz_recv.at[zz])
            total = w_z[0].astype(F32)
            for zz in range(1, ZN):
                total += w_z[zz].astype(F32)
            wg_ref[...] = total * (ALL_ROWS ** (-0.5))
            for dd in range(8):
                @pl.when(dd != d)
                def _():
                    remote(wg_ref, wg_ref, wb_send.at[dd], wb_recv, (dd, s)).start()

    backward_sib(3)
    backward_own(3)
    chip_sum(3)
    project()
    backward_sib(2)
    relay(3)
    backward_own(2)
    chip_sum(2)
    weight_x()
    finish(3)
    backward_sib(1)
    relay(2)
    weight_y()
    backward_own(1)
    chip_sum(1)
    finish(2)
    weight_z()
    backward_sib(0)
    relay(1)
    backward_own(0)
    chip_sum(0)
    finish(1)
    dq_blk[...] = (jnp.transpose(dq_acc[...]) * (0.5 * SCALE)).astype(BF).reshape(SLOTS, TOK, HEAD)
    for j in range(SLOTS):
        give_back(dq_blk.at[j], dq_ref.at[:, head_cols], f_send.at[2, j], f_recv.at[2, head], j)
    weight_all()
    relay(0)
    finish(0)

    for a, dst in ((0, dk_ref), (1, dv_ref), (2, dq_ref)):
        for h in range(HEADS):
            landed(dst.at[:, h * HEAD:(h + 1) * HEAD], f_recv.at[a, h])

    @pl.when(collector)
    def _():
        for dd in range(8):
            @pl.when(dd != d)
            def _():
                remote(wg_ref, wg_ref, wb_send.at[dd], wb_recv, (dd, s)).wait_send()

    @pl.when(jnp.logical_not(collector))
    def _():
        landed(wg_ref, wb_recv)
        remote(w_16, w_z.at[z], wz_send, wz_recv.at[z], (d, YN * d + y)).wait_send()

    def sent(src, sem):
        pltpu.make_async_copy(src, src, sem).wait()

    sent(ends_ref, e_sem.at[0])
    sent(w_part.at[:, 1 - c], ws_sem.at[0])
    for h in range(HEADS):
        @pl.when(jnp.logical_not(home[h][1]))
        def _():
            for a in range(4):
                sent(q_blk.at[0], a_send.at[a, h])

        @pl.when(h != head)
        def _():
            sent(stat.at[head], t_send.at[h])
    for j in range(SLOTS):
        @pl.when(jnp.logical_not(owner[j][1]))
        def _():
            sent(nrm_blk.at[j], n_send.at[j])
            for a in range(3):
                sent(dq_blk.at[j], f_send.at[a, j])
        for a in range(2):
            for n in range(3):
                sent(q_blk.at[0], y_send.at[a, j, n])
            sent(part_out.at[a, j], s_send.at[a, j])
            sent(part_out.at[a, j], p_send.at[a, j])
        for n in range(6):
            sent(ring_in.at[n, j], r_send.at[n, j])
    for step in range(3):
        sent(w_x.at[step], wx_send.at[step])
        sent(w_y.at[step], wy_send.at[step])


def per_device(queries, keys, values, gates, gain, out_weight, out_grad, lengths):
    ends = jnp.cumsum(lengths[0])[:, None]
    ends = jnp.broadcast_to(jnp.concatenate([ends, ends], axis=0), (8, SLOTS * TOK)).astype(jnp.int32)
    vm = pl.BlockSpec(memory_space=pltpu.VMEM)
    block = (SLOTS, TOK, HEAD)
    dma = pltpu.SemaphoreType.DMA
    scratch = [
        pltpu.VMEM((ZN * YN, TOK, HEAD), BF),
        pltpu.VMEM((ZN * YN, TOK, HEAD), BF),
        pltpu.VMEM(block, BF),
        pltpu.VMEM(block, BF),
        pltpu.VMEM((TOK, QK), BF),
        pltpu.VMEM((TOK, QK), F32),
        pltpu.VMEM((8, SLOTS * TOK), jnp.int32),
        pltpu.VMEM(block, F32),
        pltpu.VMEM((HEADS, 8, SLOTS * TOK), F32),
        pltpu.VMEM(block, BF),
        pltpu.VMEM(block, BF),
        pltpu.VMEM((TOK, QK), BF),
        pltpu.VMEM((HEAD, SLOTS * TOK), F32),
        pltpu.VMEM(block, BF),
        pltpu.VMEM((2, SLOTS, YN, TOK, HEAD), BF),
        pltpu.VMEM((2, SLOTS, YN, TOK, HEAD), BF),
        pltpu.VMEM((2, YN, TOK, HEAD), F32),
        pltpu.VMEM((2, SLOTS, YN, TOK, HEAD), BF),
        pltpu.VMEM((6, SLOTS, TOK, HEAD), BF),
        pltpu.VMEM((2, SLOTS, TOK, HEAD), BF),
        pltpu.VMEM((2, SLOTS, TOK, HEAD), BF),
        pltpu.VMEM((4, 2, 64, WIDTH), BF),
        pltpu.VMEM((4, 64, WIDTH), BF),
        pltpu.VMEM((4, 64, WIDTH), BF),
        pltpu.VMEM((3, 64, WIDTH), BF),
        pltpu.VMEM((YN, 16, WIDTH), BF),
        pltpu.VMEM((3, 16, WIDTH), BF),
        pltpu.VMEM((16, WIDTH), BF),
        pltpu.VMEM((ZN, 16, WIDTH), BF),
        dma((4, 4)), dma((4, 4)),
        dma((2, 4, 3)), dma((2, 4, 3)),
        dma((2, 4)), dma((2, 4)),
        dma((2,)),
        dma((4,)), dma((4,)),
        dma((4,)), dma((4,)),
        dma((2, 4)), dma((2, 4)),
        dma((6, 4)), dma((6, 4)),
        dma((3, 4)), dma((3, 4)),
        dma((2,)),
        dma((3,)), dma((3,)),
        dma((3,)), dma((3,)),
        dma, dma((8,)),
        dma((8,)), dma,
    ]
    return pl.pallas_call(
        layer_kernel,
        out_shape=(
            jax.ShapeDtypeStruct((TOK, WIDTH), BF),
            jax.ShapeDtypeStruct((TOK, QK), BF),
            jax.ShapeDtypeStruct((TOK, QK), BF),
            jax.ShapeDtypeStruct((TOK, QK), BF),
            jax.ShapeDtypeStruct((TOK, QK), BF),
            jax.ShapeDtypeStruct((16, WIDTH), F32),
        ),
        in_specs=[vm] * 9,
        out_specs=(vm,) * 6,
        scratch_shapes=scratch,
        compiler_params=pltpu.CompilerParams(
            collective_id=0, has_side_effects=True, vmem_limit_bytes=56 * 1024 * 1024
        ),
    )(
        queries, keys, values, gates, out_grad, out_weight,
        gain.reshape(1, QK), gain.reshape(HEADS, 1, HEAD), ends,
    )


def solution(mesh):
    rows = P(("dp", "seq"), None)

    def program(queries, keys, values, gates, gain, out_weight, out_grad, lengths):
        return jax.shard_map(
            per_device,
            mesh=mesh,
            in_specs=(rows, rows, rows, rows, P(), P(), rows, P("dp", None)),
            out_specs=(rows, rows, rows, rows, rows, P("seq", None)),
            check_vma=False,
        )(queries, keys, values, gates, gain, out_weight, out_grad, lengths)

    return program
```

```python
import jax
import jax.numpy as jnp
from jax import lax
from jax.experimental import pallas as pl
from jax.experimental.pallas import tpu as pltpu
from jax.sharding import PartitionSpec as P

TOK = 192
HEAD = 128
HEADS = 4
QK = HEAD * HEADS
WIDTH = 1024
SLOTS = 4
YN = 4
ZN = 8
CHUNK = SLOTS * TOK
PAIR = 2 * TOK
SCALE = HEAD ** (-0.5)
EPS = 1e-5
ALL_ROWS = 49152
BF = jnp.bfloat16
F32 = jnp.float32
MESH = pl.DeviceIdType.MESH
NT = (((1,), (1,)), ((), ()))
NN = (((1,), (0,)), ((), ()))


def dot(a, b, dims=NN):
    return lax.dot_general(a, b, dims, preferred_element_type=F32)


def layer_kernel(
    q_ref, k_ref, v_ref, u_hbm, og_hbm, w_hbm, gain_ref, len_ref,
    lay_ref, dq_ref, dk_ref, dv_ref, gg_out_ref, wg_ref,
    k_all, v_all, q_all, do_all, u_ref, og_ref, w_ref, gh_blk, gh_own, gg, ends_own, ends_sib, att, slope,
    q_own, k_own, v_own, do_own, place_c, begin_c,
    stat, stat_in, cen_blk, cen_in, norm_own, dq_acc, dk_acc, dv_acc, out_blk,
    w_part, w_sib, w_sum, w_xa, w_ya, w_b, w_xb, w_yb, w_16, w_z, w_fin,
    l_sem, a_send, a_recv, y_send, y_recv, s_send, s_recv, e_sem, t_send, t_recv, n_send, n_recv, m_send, m_recv,
    f_send, f_recv, ws_sem, wx_send, wx_recv, wy_send, wy_recv, wz_send, wz_recv, wb_send, wb_recv,
):
    d = lax.axis_index("dp")
    s = lax.axis_index("seq")
    x, c = d // 2, d % 2
    z, y = s // YN, s % YN
    row, head = z // HEADS, z % HEADS
    core_of_z = ((z + 1) // 2) % 2
    slot_of_z = z // 2
    right, left, across = (y + 1) % YN, (y + 3) % YN, (y + 2) % YN

    def zmap(core, j):
        return 2 * j + core if j % 2 == 0 else 2 * j + 1 - core

    def at(core, zz, yy):
        return (2 * x + core, YN * zz + yy)

    sibling = at(1 - c, z, y)
    to_right, to_left = at(c, z, right), at(c, z, left)

    def remote(src, dst, send, recv, device):
        return pltpu.make_async_remote_copy(
            src_ref=src, dst_ref=dst, send_sem=send, recv_sem=recv,
            device_id=device, device_id_type=MESH,
        )

    def landed(dst, sem):
        pltpu.make_async_copy(dst, dst, sem).wait()

    home = [(at(core_of_z, HEADS * c + h, y), (core_of_z == c) & (HEADS * c + h == z)) for h in range(HEADS)]
    owner = [(at(row, zmap(c, j), y), (row == c) & (zmap(c, j) == z)) for j in range(SLOTS)]
    own_z = [zmap(c, j) for j in range(SLOTS)]
    collector = z == d

    bar = pltpu.get_barrier_semaphore()

    def greet(device):
        pl.semaphore_signal(bar, inc=1, device_id=device, device_id_type=MESH)

    for device, mine in home + owner:
        @pl.when(jnp.logical_not(mine))
        def _():
            greet(device)
    for h in range(HEADS):
        @pl.when(h != head)
        def _():
            greet(at(c, HEADS * row + h, y))

    @pl.when(collector)
    def _():
        for zz in range(ZN):
            @pl.when(zz != z)
            def _():
                greet((d, YN * zz + y))

    @pl.when(jnp.logical_not(collector))
    def _():
        greet((z, s))

    for step in range(1, YN):
        greet(at(c, z, (y + step) % YN))
        greet((2 * ((x + step) % 4) + c, s))
    greet(sibling)

    loads = [pltpu.make_async_copy(src, dst, l_sem.at[i]) for i, (src, dst) in enumerate(
        ((w_hbm, w_ref), (og_hbm, og_ref), (u_hbm, u_ref)))]
    for load in loads:
        load.start()
    total = jnp.zeros((1, 1), jnp.int32)
    ends_own[...] = jnp.zeros_like(ends_own)
    for h in range(3):
        total = total + len_ref[:, h:h + 1]
        ends_own[h:h + 1, :] = jnp.broadcast_to(total, (1, CHUNK))
    for load in loads:
        load.wait()
    gg[...] = dot(og_ref[...], w_ref[...], NT)
    gh_own[...] = (gg[...] * u_ref[...].astype(F32) * gain_ref[...]).astype(BF)

    selfs = (home[0][1] | home[1][1] | home[2][1] | home[3][1]).astype(jnp.int32)
    pl.semaphore_wait(bar, 8 - 2 * selfs + 3 + 3 + 1 + 3 + jnp.where(collector, ZN - 1, 1))

    block = (y, slot_of_z, core_of_z)

    def scatter(a, src, dst):
        for h in range(HEADS):
            device, mine = home[h]
            cols = src.at[:, h * HEAD:(h + 1) * HEAD]

            @pl.when(mine)
            def _():
                pltpu.make_async_copy(cols, dst, a_recv.at[a, slot_of_z]).start()

            @pl.when(jnp.logical_not(mine))
            def _():
                remote(cols, dst, a_send.at[a, h], a_recv.at[a, slot_of_z], device).start()

    def scattered(a):
        for h in range(HEADS):
            @pl.when(jnp.logical_not(home[h][1]))
            def _():
                sent(gh_blk.at[0], a_send.at[a, h])

    def sent(src, sem):
        pltpu.make_async_copy(src, src, sem).wait()

    gathered = (k_all, v_all, q_all, do_all)
    HALF = TOK // 2
    low, high = pl.ds(0, HALF), pl.ds(HALF, HALF)

    near = (y, left, right, across)

    def direct(a, j):
        ref = gathered[a].at[y, j, c]
        remote(ref, ref, y_send.at[a, j, 0], y_recv.at[a, j, 0], to_right).start()
        remote(ref, ref, y_send.at[a, j, 1], y_recv.at[a, j, 1], to_left).start()

    def forward(a, j):
        ref = gathered[a].at[left, j, c]
        landed(ref, y_recv.at[a, j, 0])
        half = ref.at[low]
        remote(half, half, y_send.at[a, j, 2], y_recv.at[a, j, 2], to_right).start()
        ref = gathered[a].at[right, j, c]
        landed(ref, y_recv.at[a, j, 1])
        half = ref.at[high]
        remote(half, half, y_send.at[a, j, 3], y_recv.at[a, j, 3], to_left).start()

    def share(a, n):
        if n == 3:
            for j in range(SLOTS):
                ref = gathered[a].at[across, j, c]
                landed(ref.at[low], y_recv.at[a, j, 2])
                landed(ref.at[high], y_recv.at[a, j, 3])
        ref = gathered[a].at[near[n], :, c]
        remote(ref, ref, s_send.at[a, n], s_recv.at[a, n], sibling).start()

    def shared(a, n):
        landed(gathered[a].at[near[n], :, 1 - c], s_recv.at[a, n])

    def start_of(place, ends):
        return jnp.where(place >= ends[2], ends[2], jnp.where(
            place >= ends[1], ends[1], jnp.where(place >= ends[0], ends[0], 0)))

    def near_at(g):
        return jnp.where(g == 0, y, jnp.where(g == 1, left, jnp.where(g == 2, right, across)))

    def pair_of(ref, yy, j):
        return ref[yy, j].reshape(PAIR, HEAD)

    def pair_place(yy, j, lanes):
        first, second = (YN * zmap(core, j) + yy for core in range(2))
        return jnp.where(lanes < TOK, first * TOK, (second - 1) * TOK) + lanes

    lanes = lax.broadcasted_iota(jnp.int32, (1, PAIR), 1)

    def attend(g):
        yy = near_at(g)
        for j in range(SLOTS):
            rows = (SLOTS - j) * TOK
            queries = q_own[j * TOK:, :]
            half = dot(queries, pair_of(k_all, yy, j), NT) * (0.5 * SCALE)
            key_place = pair_place(yy, j, lanes)
            visible = (key_place <= place_c[j * TOK:, :]) & (key_place >= begin_c[j * TOK:, :])
            plus = jnp.where(visible, 1.0 + jnp.tanh(half), 0.0)
            weights = half * plus
            slope[g, j, 0:rows] = plus + weights * (2.0 - plus)
            att[j * TOK:, :] += dot(weights.astype(BF), pair_of(v_all, yy, j))

    def attend_back(g, carry):
        yy = near_at(g)
        for j in range(SLOTS):
            rows = (SLOTS - j) * TOK
            gw = dot(do_own[j * TOK:, :], pair_of(v_all, yy, j), NT)
            dq_acc[j * TOK:, :] += dot((gw * slope[g, j, 0:rows]).astype(BF), pair_of(k_all, yy, j))
        return carry

    def key_back(g):
        yy = near_at(g)
        for j in reversed(range(SLOTS)):
            rows = (j + 1) * TOK
            queries, grads_out = pair_of(q_all, yy, j), pair_of(do_all, yy, j)
            half = dot(k_own[0:rows, :], queries, NT) * (0.5 * SCALE)
            gw = dot(v_own[0:rows, :], grads_out, NT)
            place = pair_place(yy, j, lanes)
            begin = start_of(place, [ends[h:h + 1, 0:PAIR] for h in range(3)])
            key_place = place_c[0:rows, :]
            visible = (key_place <= place) & (key_place >= begin)
            plus = jnp.where(visible, 1.0 + jnp.tanh(half), 0.0)
            weights = half * plus
            dv_acc[0:rows, :] += dot(weights.astype(BF), grads_out)
            dk_acc[0:rows, :] += dot((gw * (plus + weights * (2.0 - plus))).astype(BF), queries)

    remote(ends_own, ends_sib, e_sem.at[0], e_sem.at[1], sibling).start()
    scatter(0, k_ref, k_all.at[block])
    scattered(0)
    scatter(1, v_ref, v_all.at[block])
    for j in range(SLOTS):
        landed(k_all.at[y, j, c], a_recv.at[0, j])
        direct(0, j)
    share(0, 0)
    scattered(1)
    scatter(2, q_ref, q_all.at[block])
    for j in range(SLOTS):
        landed(v_all.at[y, j, c], a_recv.at[1, j])
        direct(1, j)
    share(1, 0)
    att[...] = jnp.zeros_like(att)
    landed(ends_sib, e_sem.at[1])
    ends = jnp.where(row == c, ends_own[...], ends_sib[...])
    for j in range(SLOTS):
        k_own[j * TOK:(j + 1) * TOK, :] = k_all[y, j, c]
        v_own[j * TOK:(j + 1) * TOK, :] = v_all[y, j, c]
        place = (YN * own_z[j] + y) * TOK + lax.broadcasted_iota(jnp.int32, (TOK, 1), 0)
        place_c[j * TOK:(j + 1) * TOK, :] = place
        begin_c[j * TOK:(j + 1) * TOK, :] = start_of(place, [ends[h:h + 1, 0:1] for h in range(3)])
    for j in range(SLOTS):
        forward(0, j)
    share(0, 1)
    share(0, 2)
    scattered(2)
    scatter(3, gh_own, gh_blk.at[slot_of_z])
    for j in range(SLOTS):
        landed(q_all.at[y, j, c], a_recv.at[2, j])
        q_own[j * TOK:(j + 1) * TOK, :] = q_all[y, j, c]

    def forward_step(g, carry):
        @pl.when(g == 0)
        def _():
            shared(0, 0)
            shared(1, 0)

        @pl.when(g == 1)
        def _():
            for j in range(SLOTS):
                forward(1, j)
            share(1, 1)
            share(1, 2)
            share(0, 3)
            for a in range(2):
                shared(a, 1)

        @pl.when(g == 2)
        def _():
            for a in range(2):
                shared(a, 2)

        @pl.when(g == 3)
        def _():
            share(1, 3)
            for j in range(SLOTS):
                direct(2, j)
            share(2, 0)
            for a in range(2):
                shared(a, 3)

        attend(g)
        return carry

    lax.fori_loop(0, 4, forward_step, 0)

    head_cols = pl.ds(pl.multiple_of(head * HEAD, HEAD), HEAD)

    def give_back(src, dst, send, recv, j):
        device, mine = owner[j]

        @pl.when(mine)
        def _():
            pltpu.make_async_copy(src, dst, recv).start()

        @pl.when(jnp.logical_not(mine))
        def _():
            remote(src, dst, send, recv, device).start()

    for j in range(SLOTS):
        landed(gh_blk.at[j], a_recv.at[3, j])
    lane = lax.broadcasted_iota(jnp.int32, (TOK, HEAD), 1)
    for j in range(SLOTS):
        block_gh = gh_blk[j].astype(F32)
        block_att = att[j * TOK:(j + 1) * TOK, :]
        head_mean = jnp.mean(block_att, axis=1, keepdims=True)
        centred = block_att - head_mean
        packed = jnp.where(lane == 0, head_mean, 0.0)
        packed = jnp.where(lane == 1, jnp.sum(centred * centred, axis=1, keepdims=True), packed)
        packed = jnp.where(lane == 2, jnp.sum(block_gh * centred, axis=1, keepdims=True), packed)
        packed = jnp.where(lane == 3, jnp.sum(block_gh, axis=1, keepdims=True), packed)
        stat[head, j] = jnp.transpose(packed)[0:8]
        cen_blk[j] = centred.astype(BF)
    for h in range(HEADS):
        @pl.when(h != head)
        def _():
            remote(stat.at[head], stat.at[head], t_send.at[h], t_recv.at[head],
                   at(c, HEADS * row + h, y)).start()
    for j in range(SLOTS):
        give_back(stat.at[head, j], stat_in.at[head], m_send.at[j], m_recv.at[head], j)
    for j in range(SLOTS):
        give_back(cen_blk.at[j], cen_in.at[:, head_cols], n_send.at[j], n_recv.at[head], j)
    dq_acc[...] = jnp.zeros_like(dq_acc)
    for j in range(SLOTS):
        forward(2, j)

    def combined(parts):
        means = [part[0:1] for part in parts]
        mean = (means[0] + means[1] + means[2] + means[3]) * (1.0 / HEADS)
        square, cross, grad_sum = 0.0, 0.0, 0.0
        for part in parts:
            off = part[0:1] - mean
            square += part[1:2] + HEAD * off * off
            cross += part[2:3] + off * part[3:4]
            grad_sum += part[3:4]
        inv_std = 1.0 / jnp.sqrt(square * (1.0 / QK) + EPS)
        return [mean, inv_std, grad_sum * (1.0 / QK), cross * inv_std * (1.0 / QK)] + means

    def columns(rows):
        pad = jnp.zeros((HEAD - len(rows), TOK), F32)
        cols = jnp.transpose(jnp.concatenate(rows + [pad], axis=0))
        return [cols[:, i:i + 1] for i in range(len(rows))]

    for h in range(HEADS):
        @pl.when(h != head)
        def _():
            landed(stat.at[h], t_recv.at[h])
    for j in reversed(range(SLOTS)):
        mean_c, inv_c, gmean_c, proj_c = columns(combined([stat[h, j] for h in range(HEADS)])[:4])
        unit = (att[j * TOK:(j + 1) * TOK, :] - mean_c) * inv_c
        attn_grad = (inv_c * (gh_blk[j].astype(F32) - gmean_c - unit * proj_c)).astype(BF)
        do_all[y, j, c] = attn_grad
        do_own[j * TOK:(j + 1) * TOK, :] = attn_grad
        direct(3, j)
    share(3, 0)
    share(2, 1)
    share(2, 2)

    def project():
        for h in range(HEADS):
            landed(cen_in.at[:, h * HEAD:(h + 1) * HEAD], n_recv.at[h])
            landed(stat_in.at[h], m_recv.at[h])
        cols = columns(combined([stat_in[h] for h in range(HEADS)]))
        normed = jnp.concatenate([
            cen_in[:, h * HEAD:(h + 1) * HEAD].astype(F32) + (cols[4 + h] - cols[0]) for h in range(HEADS)
        ], axis=1) * cols[1] * gain_ref[...]
        gated = (normed * u_ref[...].astype(F32)).astype(BF)
        w_part[...] = dot(jnp.transpose(gated), og_ref[...]).astype(BF).reshape(4, 2, 64, WIDTH)
        remote(w_part.at[:, 1 - c], w_sib, ws_sem.at[0], ws_sem.at[1], sibling).start()
        norm_own[...] = normed

    def project_out():
        normed = norm_own[...]
        gated = (normed * u_ref[...].astype(F32)).astype(BF)
        gg_out_ref[...] = (gg[...] * normed).astype(BF)
        lay_ref[...] = dot(gated, w_ref[...]).astype(BF)

    HW = WIDTH // 2
    first_half, second_half = pl.ds(0, HW), pl.ds(HW, HW)

    def weight_a():
        landed(w_sib, ws_sem.at[1])
        w_sum[...] = (w_part[:, c].astype(F32) + w_sib[...].astype(F32)).astype(BF).reshape(4, YN, 16, WIDTH)
        for n in range(3):
            to = (x + n + 1) % 4
            remote(w_sum.at[to, :, :, first_half], w_xa.at[n], wx_send.at[n], wx_recv.at[n],
                   (2 * to + c, s)).start()
            to = (y + n + 1) % YN
            remote(w_sum.at[:, to, :, second_half], w_ya.at[n], wy_send.at[n], wy_recv.at[n],
                   at(c, z, to)).start()

    def weight_b():
        for n in range(3):
            landed(w_xa.at[n], wx_recv.at[n])
            landed(w_ya.at[n], wy_recv.at[n])
        w_b[0] = (w_sum[x, :, :, 0:HW].astype(F32) + w_xa[0].astype(F32) + w_xa[1].astype(F32)
                  + w_xa[2].astype(F32)).astype(BF)
        w_b[1] = (w_sum[:, y, :, HW:].astype(F32) + w_ya[0].astype(F32) + w_ya[1].astype(F32)
                  + w_ya[2].astype(F32)).astype(BF)
        for n in range(3):
            to = (y + n + 1) % YN
            remote(w_b.at[0, to], w_yb.at[n], wy_send.at[n + 3], wy_recv.at[n + 3], at(c, z, to)).start()
            to = (x + n + 1) % 4
            remote(w_b.at[1, to], w_xb.at[n], wx_send.at[n + 3], wx_recv.at[n + 3], (2 * to + c, s)).start()

    def weight_z():
        for n in range(3):
            landed(w_yb.at[n], wy_recv.at[n + 3])
            landed(w_xb.at[n], wx_recv.at[n + 3])
        w_16[:, 0:HW] = (w_b[0, y].astype(F32) + w_yb[0].astype(F32) + w_yb[1].astype(F32)
                         + w_yb[2].astype(F32)).astype(BF)
        w_16[:, HW:] = (w_b[1, x].astype(F32) + w_xb[0].astype(F32) + w_xb[1].astype(F32)
                        + w_xb[2].astype(F32)).astype(BF)

        @pl.when(jnp.logical_not(collector))
        def _():
            remote(w_16, w_z.at[z], wz_send, wz_recv.at[z], (d, YN * d + y)).start()

    def weight_all():
        @pl.when(collector)
        def _():
            w_z[z] = w_16[...]
            for zz in range(ZN):
                @pl.when(zz != z)
                def _():
                    landed(w_z.at[zz], wz_recv.at[zz])
            total = w_z[0].astype(F32)
            for zz in range(1, ZN):
                total += w_z[zz].astype(F32)
            w_fin[...] = (total * (ALL_ROWS ** (-0.5))).astype(BF)
            for dd in range(8):
                @pl.when(dd != d)
                def _():
                    remote(w_fin, w_fin, wb_send.at[dd], wb_recv, (dd, s)).start()

    lax.fori_loop(0, 4, attend_back, 0)
    for j in reversed(range(SLOTS)):
        forward(3, j)
    share(3, 1)
    share(3, 2)
    out_blk[2] = (dq_acc[...] * (0.5 * SCALE)).astype(BF).reshape(SLOTS, TOK, HEAD)
    for j in range(SLOTS):
        give_back(out_blk.at[2, j], dq_ref.at[:, head_cols], f_send.at[2, j], f_recv.at[2, head], j)
    project()
    dk_acc[...] = jnp.zeros_like(dk_acc)
    dv_acc[...] = jnp.zeros_like(dv_acc)

    def backward_step(g, carry):
        for n in range(4):
            @pl.when(g == n)
            def _():
                if n == 2:
                    weight_a()
                if n == 3:
                    share(2, 3)
                    share(3, 3)
                for a in (2, 3):
                    shared(a, n)

        key_back(g)
        return carry

    lax.fori_loop(0, 4, backward_step, 0)
    out_blk[0] = (dk_acc[...] * (0.5 * SCALE)).astype(BF).reshape(SLOTS, TOK, HEAD)
    for j in range(SLOTS):
        give_back(out_blk.at[0, j], dk_ref.at[:, head_cols], f_send.at[0, j], f_recv.at[0, head], j)
    out_blk[1] = dv_acc[...].astype(BF).reshape(SLOTS, TOK, HEAD)
    for j in range(SLOTS):
        give_back(out_blk.at[1, j], dv_ref.at[:, head_cols], f_send.at[1, j], f_recv.at[1, head], j)
    weight_b()
    weight_z()
    project_out()
    weight_all()

    @pl.when(collector)
    def _():
        for dd in range(8):
            @pl.when(dd != d)
            def _():
                sent(w_fin, wb_send.at[dd])

    @pl.when(jnp.logical_not(collector))
    def _():
        landed(w_fin, wb_recv)
        sent(w_16, wz_send)

    wg_ref[...] = w_fin[...].astype(F32)
    for a, dst in ((0, dk_ref), (1, dv_ref), (2, dq_ref)):
        for h in range(HEADS):
            landed(dst.at[:, h * HEAD:(h + 1) * HEAD], f_recv.at[a, h])
    sent(ends_own, e_sem.at[0])
    sent(w_sib, ws_sem.at[0])
    scattered(3)
    for h in range(HEADS):
        @pl.when(h != head)
        def _():
            sent(stat.at[head], t_send.at[h])
    for j in range(SLOTS):
        @pl.when(jnp.logical_not(owner[j][1]))
        def _():
            sent(cen_blk.at[j], n_send.at[j])
            sent(stat_in.at[0], m_send.at[j])
            for a in range(3):
                sent(out_blk.at[a, j], f_send.at[a, j])
        for a in range(4):
            for n in range(2):
                sent(gh_blk.at[0], y_send.at[a, j, n])
                sent(gh_blk.at[0, low], y_send.at[a, j, n + 2])
            sent(k_all.at[0, :, 0], s_send.at[a, j])
    for n in range(3):
        sent(w_xa.at[n], wx_send.at[n])
        sent(w_ya.at[n], wy_send.at[n])
        sent(w_xb.at[n], wx_send.at[n + 3])
        sent(w_yb.at[n], wy_send.at[n + 3])


def copy_kernel(*refs):
    count = len(refs) // 2
    for source, result in zip(refs[:count], refs[count:]):
        result[...] = source[...]


def per_device(queries, keys, values, gates, gain, out_weight, out_grad, lengths):
    vm = pl.BlockSpec(memory_space=pltpu.VMEM)
    anywhere = pl.BlockSpec(memory_space=pl.ANY)
    block = (SLOTS, TOK, HEAD)
    whole = (YN, SLOTS, 2, TOK, HEAD)
    own = (CHUNK, HEAD)
    dma = pltpu.SemaphoreType.DMA
    scratch = [
        pltpu.VMEM(whole, BF),
        pltpu.VMEM(whole, BF),
        pltpu.VMEM(whole, BF),
        pltpu.VMEM(whole, BF),
        pltpu.VMEM((TOK, QK), BF),
        pltpu.VMEM((TOK, WIDTH), BF),
        pltpu.VMEM((QK, WIDTH), BF),
        pltpu.VMEM(block, BF),
        pltpu.VMEM((TOK, QK), BF),
        pltpu.VMEM((TOK, QK), F32),
        pltpu.VMEM((8, CHUNK), jnp.int32),
        pltpu.VMEM((8, CHUNK), jnp.int32),
        pltpu.VMEM(own, F32),
        pltpu.VMEM((YN, SLOTS, CHUNK, PAIR), F32),
        pltpu.VMEM(own, BF),
        pltpu.VMEM(own, BF),
        pltpu.VMEM(own, BF),
        pltpu.VMEM(own, BF),
        pltpu.VMEM((CHUNK, 1), jnp.int32),
        pltpu.VMEM((CHUNK, 1), jnp.int32),
        pltpu.VMEM((HEADS, SLOTS, 8, TOK), F32),
        pltpu.VMEM((HEADS, 8, TOK), F32),
        pltpu.VMEM(block, BF),
        pltpu.VMEM((TOK, QK), BF),
        pltpu.VMEM((TOK, QK), F32),
        pltpu.VMEM(own, F32),
        pltpu.VMEM(own, F32),
        pltpu.VMEM(own, F32),
        pltpu.VMEM((3, SLOTS, TOK, HEAD), BF),
        pltpu.VMEM((4, 2, 64, WIDTH), BF),
        pltpu.VMEM((4, 64, WIDTH), BF),
        pltpu.VMEM((4, YN, 16, WIDTH), BF),
        pltpu.VMEM((3, YN, 16, WIDTH // 2), BF),
        pltpu.VMEM((3, YN, 16, WIDTH // 2), BF),
        pltpu.VMEM((2, YN, 16, WIDTH // 2), BF),
        pltpu.VMEM((3, 16, WIDTH // 2), BF),
        pltpu.VMEM((3, 16, WIDTH // 2), BF),
        pltpu.VMEM((16, WIDTH), BF),
        pltpu.VMEM((ZN, 16, WIDTH), BF),
        pltpu.VMEM((16, WIDTH), BF),
        dma((3,)),
        dma((4, 4)), dma((4, 4)),
        dma((4, 4, 4)), dma((4, 4, 4)),
        dma((4, 4)), dma((4, 4)),
        dma((2,)),
        dma((4,)), dma((4,)),
        dma((4,)), dma((4,)),
        dma((4,)), dma((4,)),
        dma((3, 4)), dma((3, 4)),
        dma((2,)),
        dma((6,)), dma((6,)),
        dma((6,)), dma((6,)),
        dma, dma((8,)),
        dma((8,)), dma,
    ]
    shapes = (
        jax.ShapeDtypeStruct((TOK, WIDTH), BF),
        jax.ShapeDtypeStruct((TOK, QK), BF),
        jax.ShapeDtypeStruct((TOK, QK), BF),
        jax.ShapeDtypeStruct((TOK, QK), BF),
        jax.ShapeDtypeStruct((TOK, QK), BF),
        jax.ShapeDtypeStruct((16, WIDTH), F32),
    )
    results = pl.pallas_call(
        layer_kernel,
        out_shape=shapes,
        in_specs=[anywhere] * 6 + [vm] * 2,
        out_specs=(vm,) * 6,
        scratch_shapes=scratch,
        compiler_params=pltpu.CompilerParams(
            collective_id=0, has_side_effects=True, vmem_limit_bytes=56 * 1024 * 1024
        ),
    )(
        queries, keys, values, gates, out_grad, out_weight,
        gain.reshape(1, QK), lengths,
    )
    return pl.pallas_call(
        copy_kernel,
        out_shape=shapes,
        in_specs=[vm] * 6,
        out_specs=(vm,) * 6,
    )(*results)


def solution(mesh):
    rows = P(("dp", "seq"), None)

    def program(queries, keys, values, gates, gain, out_weight, out_grad, lengths):
        return jax.shard_map(
            per_device,
            mesh=mesh,
            in_specs=(rows, rows, rows, rows, P(), P(), rows, P("dp", None)),
            out_specs=(rows, rows, rows, rows, rows, P("seq", None)),
            check_vma=False,
        )(queries, keys, values, gates, gain, out_weight, out_grad, lengths)

    return program
```

```python
import jax
import jax.numpy as jnp
from jax import lax
from jax.experimental import pallas as pl
from jax.experimental.pallas import tpu as pltpu
from jax.sharding import PartitionSpec as P

TOK = 192
HEAD = 128
HEADS = 4
QK = HEAD * HEADS
WIDTH = 1024
SLOTS = 4
YN = 4
ZN = 8
CHUNK = SLOTS * TOK
PAIR = 2 * TOK
SCALE = HEAD ** (-0.5)
EPS = 1e-5
ALL_ROWS = 49152
BF = jnp.bfloat16
F32 = jnp.float32
MESH = pl.DeviceIdType.MESH
NT = (((1,), (1,)), ((), ()))
NN = (((1,), (0,)), ((), ()))


def dot(a, b, dims=NN):
    return lax.dot_general(a, b, dims, preferred_element_type=F32)


def layer_kernel(
    q_ref, k_ref, v_ref, u_hbm, og_hbm, w_hbm, gain_ref, len_ref,
    lay_ref, dq_ref, dk_ref, dv_ref, gg_out_ref, wg_ref,
    k_all, v_all, q_all, do_all, u_ref, og_ref, w_ref, gh_blk, gh_own, gg, ends_own, ends_sib, att, slope,
    q_own, k_own, v_own, do_own, place_c, begin_c,
    stat, stat_in, cen_blk, cen_in, norm_own, dq_acc, dk_acc, dv_acc, out_blk,
    w_part, w_sib, w_sum, w_xa, w_ya, w_b, w_xb, w_yb, w_16, w_z, w_fin,
    l_sem, a_send, a_recv, y_send, y_recv, s_send, s_recv, e_sem, t_send, t_recv, n_send, n_recv, m_send, m_recv,
    f_send, f_recv, ws_sem, wx_send, wx_recv, wy_send, wy_recv, wz_send, wz_recv, wb_send, wb_recv,
):
    d = lax.axis_index("dp")
    s = lax.axis_index("seq")
    x, c = d // 2, d % 2
    z, y = s // YN, s % YN
    row, head = z // HEADS, z % HEADS
    core_of_z = ((z + 1) // 2) % 2
    slot_of_z = z // 2
    right, left, across = (y + 1) % YN, (y + 3) % YN, (y + 2) % YN

    def zmap(core, j):
        return 2 * j + core if j % 2 == 0 else 2 * j + 1 - core

    def at(core, zz, yy):
        return (2 * x + core, YN * zz + yy)

    sibling = at(1 - c, z, y)
    to_right, to_left = at(c, z, right), at(c, z, left)

    def remote(src, dst, send, recv, device):
        return pltpu.make_async_remote_copy(
            src_ref=src, dst_ref=dst, send_sem=send, recv_sem=recv,
            device_id=device, device_id_type=MESH,
        )

    def landed(dst, sem):
        pltpu.make_async_copy(dst, dst, sem).wait()

    home = [(at(core_of_z, HEADS * c + h, y), (core_of_z == c) & (HEADS * c + h == z)) for h in range(HEADS)]
    owner = [(at(row, zmap(c, j), y), (row == c) & (zmap(c, j) == z)) for j in range(SLOTS)]
    own_z = [zmap(c, j) for j in range(SLOTS)]
    collector = z == d

    bar = pltpu.get_barrier_semaphore()

    def greet(device):
        pl.semaphore_signal(bar, inc=1, device_id=device, device_id_type=MESH)

    for device, mine in home + owner:
        @pl.when(jnp.logical_not(mine))
        def _():
            greet(device)
    for h in range(HEADS):
        @pl.when(h != head)
        def _():
            greet(at(c, HEADS * row + h, y))

    @pl.when(collector)
    def _():
        for zz in range(ZN):
            @pl.when(zz != z)
            def _():
                greet((d, YN * zz + y))

    @pl.when(jnp.logical_not(collector))
    def _():
        greet((z, s))

    for step in range(1, YN):
        greet(at(c, z, (y + step) % YN))
        greet((2 * ((x + step) % 4) + c, s))
    greet(sibling)

    loads = [pltpu.make_async_copy(src, dst, l_sem.at[i]) for i, (src, dst) in enumerate(
        ((w_hbm, w_ref), (og_hbm, og_ref), (u_hbm, u_ref)))]
    for load in loads:
        load.start()
    total = jnp.zeros((1, 1), jnp.int32)
    ends_own[...] = jnp.zeros_like(ends_own)
    for h in range(3):
        total = total + len_ref[:, h:h + 1]
        ends_own[h:h + 1, :] = jnp.broadcast_to(total, (1, CHUNK))
    for load in loads:
        load.wait()
    gg[...] = dot(og_ref[...], w_ref[...], NT)
    gh_own[...] = (gg[...] * u_ref[...].astype(F32) * gain_ref[...]).astype(BF)

    selfs = (home[0][1] | home[1][1] | home[2][1] | home[3][1]).astype(jnp.int32)
    pl.semaphore_wait(bar, 8 - 2 * selfs + 3 + 3 + 1 + 3 + jnp.where(collector, ZN - 1, 1))

    block = (y, slot_of_z, core_of_z)

    def scatter(a, src, dst):
        for h in range(HEADS):
            device, mine = home[h]
            cols = src.at[:, h * HEAD:(h + 1) * HEAD]

            @pl.when(mine)
            def _():
                pltpu.make_async_copy(cols, dst, a_recv.at[a, slot_of_z]).start()

            @pl.when(jnp.logical_not(mine))
            def _():
                remote(cols, dst, a_send.at[a, h], a_recv.at[a, slot_of_z], device).start()

    def scattered(a):
        for h in range(HEADS):
            @pl.when(jnp.logical_not(home[h][1]))
            def _():
                sent(gh_blk.at[0], a_send.at[a, h])

    def sent(src, sem):
        pltpu.make_async_copy(src, src, sem).wait()

    gathered = (k_all, v_all, q_all, do_all)
    HALF = TOK // 2
    low, high = pl.ds(0, HALF), pl.ds(HALF, HALF)

    near = (y, left, right, across)

    def direct(a, j):
        ref = gathered[a].at[y, j, c]
        remote(ref, ref, y_send.at[a, j, 0], y_recv.at[a, j, 0], to_right).start()
        remote(ref, ref, y_send.at[a, j, 1], y_recv.at[a, j, 1], to_left).start()

    def forward(a, j):
        ref = gathered[a].at[left, j, c]
        landed(ref, y_recv.at[a, j, 0])
        half = ref.at[low]
        remote(half, half, y_send.at[a, j, 2], y_recv.at[a, j, 2], to_right).start()
        ref = gathered[a].at[right, j, c]
        landed(ref, y_recv.at[a, j, 1])
        half = ref.at[high]
        remote(half, half, y_send.at[a, j, 3], y_recv.at[a, j, 3], to_left).start()

    def share(a, n):
        if n == 3:
            for j in range(SLOTS):
                ref = gathered[a].at[across, j, c]
                landed(ref.at[low], y_recv.at[a, j, 2])
                landed(ref.at[high], y_recv.at[a, j, 3])
        ref = gathered[a].at[near[n], :, c]
        remote(ref, ref, s_send.at[a, n], s_recv.at[a, n], sibling).start()

    def shared(a, n):
        landed(gathered[a].at[near[n], :, 1 - c], s_recv.at[a, n])

    def start_of(place, ends):
        return jnp.where(place >= ends[2], ends[2], jnp.where(
            place >= ends[1], ends[1], jnp.where(place >= ends[0], ends[0], 0)))

    def near_at(g):
        return jnp.where(g == 0, y, jnp.where(g == 1, left, jnp.where(g == 2, right, across)))

    def pair_of(ref, yy, j):
        return ref[yy, j].reshape(PAIR, HEAD)

    def pair_place(yy, j, lanes):
        first, second = (YN * zmap(core, j) + yy for core in range(2))
        return jnp.where(lanes < TOK, first * TOK, (second - 1) * TOK) + lanes

    lanes = lax.broadcasted_iota(jnp.int32, (1, PAIR), 1)

    def attend(g):
        yy = near_at(g)
        for j in range(SLOTS):
            rows = (SLOTS - j) * TOK
            queries = q_own[j * TOK:, :]
            half = dot(queries, pair_of(k_all, yy, j), NT) * (0.5 * SCALE)
            key_place = pair_place(yy, j, lanes)
            visible = (key_place <= place_c[j * TOK:, :]) & (key_place >= begin_c[j * TOK:, :])
            plus = jnp.where(visible, 1.0 + jnp.tanh(half), 0.0)
            weights = half * plus
            slope[g, j, 0:rows] = plus + weights * (2.0 - plus)
            att[j * TOK:, :] += dot(weights.astype(BF), pair_of(v_all, yy, j))

    def attend_back(g, carry):
        yy = near_at(g)

        @pl.when(g == 2)
        def _():
            project()

        @pl.when(g == 3)
        def _():
            for j in reversed(range(SLOTS)):
                forward(3, j)
            share(3, 1)
            share(3, 2)

        for j in range(SLOTS):
            rows = (SLOTS - j) * TOK
            gw = dot(do_own[j * TOK:, :], pair_of(v_all, yy, j), NT)
            dq_acc[j * TOK:, :] += dot((gw * slope[g, j, 0:rows]).astype(BF), pair_of(k_all, yy, j))
        return carry

    def key_back(g):
        yy = near_at(g)
        for j in reversed(range(SLOTS)):
            rows = (j + 1) * TOK
            queries, grads_out = pair_of(q_all, yy, j), pair_of(do_all, yy, j)
            half = dot(k_own[0:rows, :], queries, NT) * (0.5 * SCALE)
            gw = dot(v_own[0:rows, :], grads_out, NT)
            place = pair_place(yy, j, lanes)
            begin = start_of(place, [ends[h:h + 1, 0:PAIR] for h in range(3)])
            key_place = place_c[0:rows, :]
            visible = (key_place <= place) & (key_place >= begin)
            plus = jnp.where(visible, 1.0 + jnp.tanh(half), 0.0)
            weights = half * plus
            dv_acc[0:rows, :] += dot(weights.astype(BF), grads_out)
            dk_acc[0:rows, :] += dot((gw * (plus + weights * (2.0 - plus))).astype(BF), queries)

    remote(ends_own, ends_sib, e_sem.at[0], e_sem.at[1], sibling).start()
    scatter(0, k_ref, k_all.at[block])
    scattered(0)
    scatter(1, v_ref, v_all.at[block])
    for j in range(SLOTS):
        landed(k_all.at[y, j, c], a_recv.at[0, j])
        direct(0, j)
    share(0, 0)
    scattered(1)
    scatter(2, q_ref, q_all.at[block])
    for j in range(SLOTS):
        landed(v_all.at[y, j, c], a_recv.at[1, j])
        direct(1, j)
    share(1, 0)
    att[...] = jnp.zeros_like(att)
    landed(ends_sib, e_sem.at[1])
    ends = jnp.where(row == c, ends_own[...], ends_sib[...])
    for j in range(SLOTS):
        k_own[j * TOK:(j + 1) * TOK, :] = k_all[y, j, c]
        v_own[j * TOK:(j + 1) * TOK, :] = v_all[y, j, c]
        place = (YN * own_z[j] + y) * TOK + lax.broadcasted_iota(jnp.int32, (TOK, 1), 0)
        place_c[j * TOK:(j + 1) * TOK, :] = place
        begin_c[j * TOK:(j + 1) * TOK, :] = start_of(place, [ends[h:h + 1, 0:1] for h in range(3)])
    for j in range(SLOTS):
        forward(0, j)
    share(0, 1)
    share(0, 2)
    scattered(2)
    scatter(3, gh_own, gh_blk.at[slot_of_z])
    for j in range(SLOTS):
        landed(q_all.at[y, j, c], a_recv.at[2, j])
        q_own[j * TOK:(j + 1) * TOK, :] = q_all[y, j, c]

    def forward_step(g, carry):
        @pl.when(g == 0)
        def _():
            shared(0, 0)
            shared(1, 0)

        @pl.when(g == 1)
        def _():
            for j in range(SLOTS):
                forward(1, j)
            share(1, 1)
            share(1, 2)
            share(0, 3)
            for a in range(2):
                shared(a, 1)

        @pl.when(g == 2)
        def _():
            for a in range(2):
                shared(a, 2)

        @pl.when(g == 3)
        def _():
            share(1, 3)
            for j in range(SLOTS):
                direct(2, j)
            share(2, 0)
            for a in range(2):
                shared(a, 3)

        attend(g)
        return carry

    lax.fori_loop(0, 4, forward_step, 0)

    head_cols = pl.ds(pl.multiple_of(head * HEAD, HEAD), HEAD)

    def give_back(src, dst, send, recv, j):
        device, mine = owner[j]

        @pl.when(mine)
        def _():
            pltpu.make_async_copy(src, dst, recv).start()

        @pl.when(jnp.logical_not(mine))
        def _():
            remote(src, dst, send, recv, device).start()

    for j in range(SLOTS):
        landed(gh_blk.at[j], a_recv.at[3, j])
    lane = lax.broadcasted_iota(jnp.int32, (TOK, HEAD), 1)
    for j in range(SLOTS):
        block_gh = gh_blk[j].astype(F32)
        block_att = att[j * TOK:(j + 1) * TOK, :]
        head_mean = jnp.mean(block_att, axis=1, keepdims=True)
        centred = block_att - head_mean
        packed = jnp.where(lane == 0, head_mean, 0.0)
        packed = jnp.where(lane == 1, jnp.sum(centred * centred, axis=1, keepdims=True), packed)
        packed = jnp.where(lane == 2, jnp.sum(block_gh * centred, axis=1, keepdims=True), packed)
        packed = jnp.where(lane == 3, jnp.sum(block_gh, axis=1, keepdims=True), packed)
        stat[head, j] = jnp.transpose(packed)[0:8]
        cen_blk[j] = centred.astype(BF)
    for h in range(HEADS):
        @pl.when(h != head)
        def _():
            remote(stat.at[head], stat.at[head], t_send.at[h], t_recv.at[head],
                   at(c, HEADS * row + h, y)).start()
    for j in range(SLOTS):
        give_back(stat.at[head, j], stat_in.at[head], m_send.at[j], m_recv.at[head], j)
    for j in range(SLOTS):
        give_back(cen_blk.at[j], cen_in.at[:, head_cols], n_send.at[j], n_recv.at[head], j)
    dq_acc[...] = jnp.zeros_like(dq_acc)
    for j in range(SLOTS):
        forward(2, j)

    def combined(parts):
        means = [part[0:1] for part in parts]
        mean = (means[0] + means[1] + means[2] + means[3]) * (1.0 / HEADS)
        square, cross, grad_sum = 0.0, 0.0, 0.0
        for part in parts:
            off = part[0:1] - mean
            square += part[1:2] + HEAD * off * off
            cross += part[2:3] + off * part[3:4]
            grad_sum += part[3:4]
        inv_std = 1.0 / jnp.sqrt(square * (1.0 / QK) + EPS)
        return [mean, inv_std, grad_sum * (1.0 / QK), cross * inv_std * (1.0 / QK)] + means

    def columns(rows):
        pad = jnp.zeros((HEAD - len(rows), TOK), F32)
        cols = jnp.transpose(jnp.concatenate(rows + [pad], axis=0))
        return [cols[:, i:i + 1] for i in range(len(rows))]

    for h in range(HEADS):
        @pl.when(h != head)
        def _():
            landed(stat.at[h], t_recv.at[h])
    for j in reversed(range(SLOTS)):
        mean_c, inv_c, gmean_c, proj_c = columns(combined([stat[h, j] for h in range(HEADS)])[:4])
        unit = (att[j * TOK:(j + 1) * TOK, :] - mean_c) * inv_c
        attn_grad = (inv_c * (gh_blk[j].astype(F32) - gmean_c - unit * proj_c)).astype(BF)
        do_all[y, j, c] = attn_grad
        do_own[j * TOK:(j + 1) * TOK, :] = attn_grad
        direct(3, j)
    share(3, 0)
    share(2, 1)
    share(2, 2)

    def project():
        for h in range(HEADS):
            landed(cen_in.at[:, h * HEAD:(h + 1) * HEAD], n_recv.at[h])
            landed(stat_in.at[h], m_recv.at[h])
        cols = columns(combined([stat_in[h] for h in range(HEADS)]))
        normed = jnp.concatenate([
            cen_in[:, h * HEAD:(h + 1) * HEAD].astype(F32) + (cols[4 + h] - cols[0]) for h in range(HEADS)
        ], axis=1) * cols[1] * gain_ref[...]
        gated = (normed * u_ref[...].astype(F32)).astype(BF)
        w_part[...] = dot(jnp.transpose(gated), og_ref[...]).astype(BF).reshape(4, 2, 64, WIDTH)
        remote(w_part.at[:, 1 - c], w_sib, ws_sem.at[0], ws_sem.at[1], sibling).start()
        norm_own[...] = normed

    def project_out():
        normed = norm_own[...]
        gated = (normed * u_ref[...].astype(F32)).astype(BF)
        gg_out_ref[...] = (gg[...] * normed).astype(BF)
        lay_ref[...] = dot(gated, w_ref[...]).astype(BF)

    HW = WIDTH // 2
    first_half, second_half = pl.ds(0, HW), pl.ds(HW, HW)

    def weight_a():
        landed(w_sib, ws_sem.at[1])
        w_sum[...] = (w_part[:, c].astype(F32) + w_sib[...].astype(F32)).astype(BF).reshape(4, YN, 16, WIDTH)
        for n in range(3):
            to = (x + n + 1) % 4
            remote(w_sum.at[to, :, :, first_half], w_xa.at[n], wx_send.at[n], wx_recv.at[n],
                   (2 * to + c, s)).start()
            to = (y + n + 1) % YN
            remote(w_sum.at[:, to, :, second_half], w_ya.at[n], wy_send.at[n], wy_recv.at[n],
                   at(c, z, to)).start()

    def weight_b():
        for n in range(3):
            landed(w_xa.at[n], wx_recv.at[n])
            landed(w_ya.at[n], wy_recv.at[n])
        w_b[0] = (w_sum[x, :, :, 0:HW].astype(F32) + w_xa[0].astype(F32) + w_xa[1].astype(F32)
                  + w_xa[2].astype(F32)).astype(BF)
        w_b[1] = (w_sum[:, y, :, HW:].astype(F32) + w_ya[0].astype(F32) + w_ya[1].astype(F32)
                  + w_ya[2].astype(F32)).astype(BF)
        for n in range(3):
            to = (y + n + 1) % YN
            remote(w_b.at[0, to], w_yb.at[n], wy_send.at[n + 3], wy_recv.at[n + 3], at(c, z, to)).start()
            to = (x + n + 1) % 4
            remote(w_b.at[1, to], w_xb.at[n], wx_send.at[n + 3], wx_recv.at[n + 3], (2 * to + c, s)).start()

    def weight_z():
        for n in range(3):
            landed(w_yb.at[n], wy_recv.at[n + 3])
            landed(w_xb.at[n], wx_recv.at[n + 3])
        w_16[:, 0:HW] = (w_b[0, y].astype(F32) + w_yb[0].astype(F32) + w_yb[1].astype(F32)
                         + w_yb[2].astype(F32)).astype(BF)
        w_16[:, HW:] = (w_b[1, x].astype(F32) + w_xb[0].astype(F32) + w_xb[1].astype(F32)
                        + w_xb[2].astype(F32)).astype(BF)

        @pl.when(jnp.logical_not(collector))
        def _():
            remote(w_16, w_z.at[z], wz_send, wz_recv.at[z], (d, YN * d + y)).start()

    def weight_all():
        @pl.when(collector)
        def _():
            w_z[z] = w_16[...]
            for zz in range(ZN):
                @pl.when(zz != z)
                def _():
                    landed(w_z.at[zz], wz_recv.at[zz])
            total = w_z[0].astype(F32)
            for zz in range(1, ZN):
                total += w_z[zz].astype(F32)
            w_fin[...] = (total * (ALL_ROWS ** (-0.5))).astype(BF)
            for dd in range(8):
                @pl.when(dd != d)
                def _():
                    remote(w_fin, w_fin, wb_send.at[dd], wb_recv, (dd, s)).start()

    lax.fori_loop(0, 4, attend_back, 0)
    out_blk[2] = (dq_acc[...] * (0.5 * SCALE)).astype(BF).reshape(SLOTS, TOK, HEAD)
    for j in range(SLOTS):
        give_back(out_blk.at[2, j], dq_ref.at[:, head_cols], f_send.at[2, j], f_recv.at[2, head], j)
    weight_a()
    dk_acc[...] = jnp.zeros_like(dk_acc)
    dv_acc[...] = jnp.zeros_like(dv_acc)

    def backward_step(g, carry):
        for n in range(4):
            @pl.when(g == n)
            def _():
                if n == 2:
                    share(2, 3)
                    share(3, 3)
                    weight_b()
                for a in (2, 3):
                    shared(a, n)

        key_back(g)
        return carry

    lax.fori_loop(0, 4, backward_step, 0)
    weight_z()
    out_blk[0] = (dk_acc[...] * (0.5 * SCALE)).astype(BF).reshape(SLOTS, TOK, HEAD)
    for j in range(SLOTS):
        give_back(out_blk.at[0, j], dk_ref.at[:, head_cols], f_send.at[0, j], f_recv.at[0, head], j)
    out_blk[1] = dv_acc[...].astype(BF).reshape(SLOTS, TOK, HEAD)
    for j in range(SLOTS):
        give_back(out_blk.at[1, j], dv_ref.at[:, head_cols], f_send.at[1, j], f_recv.at[1, head], j)
    project_out()
    weight_all()

    @pl.when(collector)
    def _():
        for dd in range(8):
            @pl.when(dd != d)
            def _():
                sent(w_fin, wb_send.at[dd])

    @pl.when(jnp.logical_not(collector))
    def _():
        landed(w_fin, wb_recv)
        sent(w_16, wz_send)

    wg_ref[...] = w_fin[...].astype(F32)
    for a, dst in ((0, dk_ref), (1, dv_ref), (2, dq_ref)):
        for h in range(HEADS):
            landed(dst.at[:, h * HEAD:(h + 1) * HEAD], f_recv.at[a, h])
    sent(ends_own, e_sem.at[0])
    sent(w_sib, ws_sem.at[0])
    scattered(3)
    for h in range(HEADS):
        @pl.when(h != head)
        def _():
            sent(stat.at[head], t_send.at[h])
    for j in range(SLOTS):
        @pl.when(jnp.logical_not(owner[j][1]))
        def _():
            sent(cen_blk.at[j], n_send.at[j])
            sent(stat_in.at[0], m_send.at[j])
            for a in range(3):
                sent(out_blk.at[a, j], f_send.at[a, j])
        for a in range(4):
            for n in range(2):
                sent(gh_blk.at[0], y_send.at[a, j, n])
                sent(gh_blk.at[0, low], y_send.at[a, j, n + 2])
            sent(k_all.at[0, :, 0], s_send.at[a, j])
    for n in range(3):
        sent(w_xa.at[n], wx_send.at[n])
        sent(w_ya.at[n], wy_send.at[n])
        sent(w_xb.at[n], wx_send.at[n + 3])
        sent(w_yb.at[n], wy_send.at[n + 3])


def copy_kernel(*refs):
    count = len(refs) // 2
    for source, result in zip(refs[:count], refs[count:]):
        result[...] = source[...]


def per_device(queries, keys, values, gates, gain, out_weight, out_grad, lengths):
    vm = pl.BlockSpec(memory_space=pltpu.VMEM)
    anywhere = pl.BlockSpec(memory_space=pl.ANY)
    block = (SLOTS, TOK, HEAD)
    whole = (YN, SLOTS, 2, TOK, HEAD)
    own = (CHUNK, HEAD)
    dma = pltpu.SemaphoreType.DMA
    scratch = [
        pltpu.VMEM(whole, BF),
        pltpu.VMEM(whole, BF),
        pltpu.VMEM(whole, BF),
        pltpu.VMEM(whole, BF),
        pltpu.VMEM((TOK, QK), BF),
        pltpu.VMEM((TOK, WIDTH), BF),
        pltpu.VMEM((QK, WIDTH), BF),
        pltpu.VMEM(block, BF),
        pltpu.VMEM((TOK, QK), BF),
        pltpu.VMEM((TOK, QK), F32),
        pltpu.VMEM((8, CHUNK), jnp.int32),
        pltpu.VMEM((8, CHUNK), jnp.int32),
        pltpu.VMEM(own, F32),
        pltpu.VMEM((YN, SLOTS, CHUNK, PAIR), F32),
        pltpu.VMEM(own, BF),
        pltpu.VMEM(own, BF),
        pltpu.VMEM(own, BF),
        pltpu.VMEM(own, BF),
        pltpu.VMEM((CHUNK, 1), jnp.int32),
        pltpu.VMEM((CHUNK, 1), jnp.int32),
        pltpu.VMEM((HEADS, SLOTS, 8, TOK), F32),
        pltpu.VMEM((HEADS, 8, TOK), F32),
        pltpu.VMEM(block, BF),
        pltpu.VMEM((TOK, QK), BF),
        pltpu.VMEM((TOK, QK), F32),
        pltpu.VMEM(own, F32),
        pltpu.VMEM(own, F32),
        pltpu.VMEM(own, F32),
        pltpu.VMEM((3, SLOTS, TOK, HEAD), BF),
        pltpu.VMEM((4, 2, 64, WIDTH), BF),
        pltpu.VMEM((4, 64, WIDTH), BF),
        pltpu.VMEM((4, YN, 16, WIDTH), BF),
        pltpu.VMEM((3, YN, 16, WIDTH // 2), BF),
        pltpu.VMEM((3, YN, 16, WIDTH // 2), BF),
        pltpu.VMEM((2, YN, 16, WIDTH // 2), BF),
        pltpu.VMEM((3, 16, WIDTH // 2), BF),
        pltpu.VMEM((3, 16, WIDTH // 2), BF),
        pltpu.VMEM((16, WIDTH), BF),
        pltpu.VMEM((ZN, 16, WIDTH), BF),
        pltpu.VMEM((16, WIDTH), BF),
        dma((3,)),
        dma((4, 4)), dma((4, 4)),
        dma((4, 4, 4)), dma((4, 4, 4)),
        dma((4, 4)), dma((4, 4)),
        dma((2,)),
        dma((4,)), dma((4,)),
        dma((4,)), dma((4,)),
        dma((4,)), dma((4,)),
        dma((3, 4)), dma((3, 4)),
        dma((2,)),
        dma((6,)), dma((6,)),
        dma((6,)), dma((6,)),
        dma, dma((8,)),
        dma((8,)), dma,
    ]
    shapes = (
        jax.ShapeDtypeStruct((TOK, WIDTH), BF),
        jax.ShapeDtypeStruct((TOK, QK), BF),
        jax.ShapeDtypeStruct((TOK, QK), BF),
        jax.ShapeDtypeStruct((TOK, QK), BF),
        jax.ShapeDtypeStruct((TOK, QK), BF),
        jax.ShapeDtypeStruct((16, WIDTH), F32),
    )
    results = pl.pallas_call(
        layer_kernel,
        out_shape=shapes,
        in_specs=[anywhere] * 6 + [vm] * 2,
        out_specs=(vm,) * 6,
        scratch_shapes=scratch,
        compiler_params=pltpu.CompilerParams(
            collective_id=0, has_side_effects=True, vmem_limit_bytes=56 * 1024 * 1024
        ),
    )(
        queries, keys, values, gates, out_grad, out_weight,
        gain.reshape(1, QK), lengths,
    )
    return pl.pallas_call(
        copy_kernel,
        out_shape=shapes,
        in_specs=[vm] * 6,
        out_specs=(vm,) * 6,
    )(*results)


def solution(mesh):
    rows = P(("dp", "seq"), None)

    def program(queries, keys, values, gates, gain, out_weight, out_grad, lengths):
        return jax.shard_map(
            per_device,
            mesh=mesh,
            in_specs=(rows, rows, rows, rows, P(), P(), rows, P("dp", None)),
            out_specs=(rows, rows, rows, rows, rows, P("seq", None)),
            check_vma=False,
        )(queries, keys, values, gates, gain, out_weight, out_grad, lengths)

    return program
```

```python
import jax
import jax.numpy as jnp
from jax import lax
from jax.experimental import pallas as pl
from jax.experimental.pallas import tpu as pltpu
from jax.sharding import PartitionSpec as P

TOK = 192
HEAD = 128
HEADS = 4
QK = HEAD * HEADS
WIDTH = 1024
SLOTS = 4
YN = 4
ZN = 8
CHUNK = SLOTS * TOK
PAIR = 2 * TOK
SCALE = HEAD ** (-0.5)
EPS = 1e-5
ALL_ROWS = 49152
BF = jnp.bfloat16
F32 = jnp.float32
MESH = pl.DeviceIdType.MESH
NT = (((1,), (1,)), ((), ()))
NN = (((1,), (0,)), ((), ()))


def dot(a, b, dims=NN):
    return lax.dot_general(a, b, dims, preferred_element_type=F32)


def layer_kernel(
    q_ref, k_ref, v_ref, u_hbm, og_hbm, w_hbm, gain_ref, len_ref,
    lay_ref, dq_ref, dk_ref, dv_ref, gg_out_ref, wg_ref,
    k_all, v_all, q_all, do_all, u_ref, og_ref, w_ref, gh_blk, gh_own, gg, ends_own, ends_sib, att, slope,
    q_own, k_own, v_own, do_own, place_c, begin_c,
    stat, stat_in, cen_blk, cen_in, norm_own, dq_acc, dk_acc, dv_acc, out_blk,
    w_part, w_sib, w_sum, w_xa, w_ya, w_b, w_xb, w_yb, w_16, w_z, w_fin,
    l_sem, a_send, a_recv, y_send, y_recv, s_send, s_recv, e_sem, t_send, t_recv, n_send, n_recv, m_send, m_recv,
    f_send, f_recv, ws_sem, wx_send, wx_recv, wy_send, wy_recv, wz_send, wz_recv, wb_send, wb_recv,
):
    d = lax.axis_index("dp")
    s = lax.axis_index("seq")
    x, c = d // 2, d % 2
    z, y = s // YN, s % YN
    row, head = z // HEADS, z % HEADS
    core_of_z = ((z + 1) // 2) % 2
    slot_of_z = z // 2
    right, left, across = (y + 1) % YN, (y + 3) % YN, (y + 2) % YN

    def zmap(core, j):
        return 2 * j + core if j % 2 == 0 else 2 * j + 1 - core

    def at(core, zz, yy):
        return (2 * x + core, YN * zz + yy)

    sibling = at(1 - c, z, y)
    to_right, to_left = at(c, z, right), at(c, z, left)

    def remote(src, dst, send, recv, device):
        return pltpu.make_async_remote_copy(
            src_ref=src, dst_ref=dst, send_sem=send, recv_sem=recv,
            device_id=device, device_id_type=MESH,
        )

    def landed(dst, sem):
        pltpu.make_async_copy(dst, dst, sem).wait()

    home = [(at(core_of_z, HEADS * c + h, y), (core_of_z == c) & (HEADS * c + h == z)) for h in range(HEADS)]
    owner = [(at(row, zmap(c, j), y), (row == c) & (zmap(c, j) == z)) for j in range(SLOTS)]
    own_z = [zmap(c, j) for j in range(SLOTS)]
    collector = z == d

    bar = pltpu.get_barrier_semaphore()

    def greet(device):
        pl.semaphore_signal(bar, inc=1, device_id=device, device_id_type=MESH)

    for device, mine in home + owner:
        @pl.when(jnp.logical_not(mine))
        def _():
            greet(device)
    for h in range(HEADS):
        @pl.when(h != head)
        def _():
            greet(at(c, HEADS * row + h, y))

    @pl.when(collector)
    def _():
        for zz in range(ZN):
            @pl.when(zz != z)
            def _():
                greet((d, YN * zz + y))

    @pl.when(jnp.logical_not(collector))
    def _():
        greet((z, s))

    for step in range(1, YN):
        greet(at(c, z, (y + step) % YN))
        greet((2 * ((x + step) % 4) + c, s))
    greet(sibling)

    loads = [pltpu.make_async_copy(src, dst, l_sem.at[i]) for i, (src, dst) in enumerate(
        ((w_hbm, w_ref), (og_hbm, og_ref), (u_hbm, u_ref)))]
    for load in loads:
        load.start()
    total = jnp.zeros((1, 1), jnp.int32)
    ends_own[...] = jnp.zeros_like(ends_own)
    for h in range(3):
        total = total + len_ref[:, h:h + 1]
        ends_own[h:h + 1, :] = jnp.broadcast_to(total, (1, CHUNK))
    for load in loads:
        load.wait()
    gg[...] = dot(og_ref[...], w_ref[...], NT)
    gh_own[...] = (gg[...] * u_ref[...].astype(F32) * gain_ref[...]).astype(BF)

    selfs = (home[0][1] | home[1][1] | home[2][1] | home[3][1]).astype(jnp.int32)
    pl.semaphore_wait(bar, 8 - 2 * selfs + 3 + 3 + 1 + 3 + jnp.where(collector, ZN - 1, 1))

    block = (y, slot_of_z, core_of_z)

    def scatter(a, src, dst):
        for h in range(HEADS):
            device, mine = home[h]
            cols = src.at[:, h * HEAD:(h + 1) * HEAD]

            @pl.when(mine)
            def _():
                pltpu.make_async_copy(cols, dst, a_recv.at[a, slot_of_z]).start()

            @pl.when(jnp.logical_not(mine))
            def _():
                remote(cols, dst, a_send.at[a, h], a_recv.at[a, slot_of_z], device).start()

    def scattered(a):
        for h in range(HEADS):
            @pl.when(jnp.logical_not(home[h][1]))
            def _():
                sent(gh_blk.at[0], a_send.at[a, h])

    def sent(src, sem):
        pltpu.make_async_copy(src, src, sem).wait()

    gathered = (k_all, v_all, q_all, do_all)
    HALF = TOK // 2
    low, high = pl.ds(0, HALF), pl.ds(HALF, HALF)

    near = (y, left, right, across)

    def direct(a, j):
        ref = gathered[a].at[y, j, c]
        remote(ref, ref, y_send.at[a, j, 0], y_recv.at[a, j, 0], to_right).start()
        remote(ref, ref, y_send.at[a, j, 1], y_recv.at[a, j, 1], to_left).start()

    def forward(a, j):
        ref = gathered[a].at[left, j, c]
        landed(ref, y_recv.at[a, j, 0])
        half = ref.at[low]
        remote(half, half, y_send.at[a, j, 2], y_recv.at[a, j, 2], to_right).start()
        ref = gathered[a].at[right, j, c]
        landed(ref, y_recv.at[a, j, 1])
        half = ref.at[high]
        remote(half, half, y_send.at[a, j, 3], y_recv.at[a, j, 3], to_left).start()

    def share(a, n):
        if n == 3:
            for j in range(SLOTS):
                ref = gathered[a].at[across, j, c]
                landed(ref.at[low], y_recv.at[a, j, 2])
                landed(ref.at[high], y_recv.at[a, j, 3])
        ref = gathered[a].at[near[n], :, c]
        remote(ref, ref, s_send.at[a, n], s_recv.at[a, n], sibling).start()

    def shared(a, n):
        landed(gathered[a].at[near[n], :, 1 - c], s_recv.at[a, n])

    def start_of(place, ends):
        return jnp.where(place >= ends[2], ends[2], jnp.where(
            place >= ends[1], ends[1], jnp.where(place >= ends[0], ends[0], 0)))

    def near_at(g):
        return jnp.where(g == 0, y, jnp.where(g == 1, left, jnp.where(g == 2, right, across)))

    def pair_of(ref, yy, j):
        return ref[yy, j].reshape(PAIR, HEAD)

    def pair_place(yy, j, lanes):
        first, second = (YN * zmap(core, j) + yy for core in range(2))
        return jnp.where(lanes < TOK, first * TOK, (second - 1) * TOK) + lanes

    lanes = lax.broadcasted_iota(jnp.int32, (1, PAIR), 1)

    def attend(g):
        yy = near_at(g)
        for j in range(SLOTS):
            rows = (SLOTS - j) * TOK
            queries = q_own[j * TOK:, :]
            score = dot(queries, pair_of(k_all, yy, j), NT) * SCALE
            key_place = pair_place(yy, j, lanes)
            visible = (key_place <= place_c[j * TOK:, :]) & (key_place >= begin_c[j * TOK:, :])
            gate = jnp.where(visible, jax.nn.sigmoid(score), 0.0)
            weights = score * gate
            slope[g, j, 0:rows] = gate + weights * (1.0 - gate)
            att[j * TOK:, :] += dot(weights.astype(BF), pair_of(v_all, yy, j))

    def attend_back(g, carry):
        yy = near_at(g)

        @pl.when(g == 2)
        def _():
            project()

        @pl.when(g == 3)
        def _():
            for j in reversed(range(SLOTS)):
                forward(3, j)
            share(3, 1)
            share(3, 2)

        for j in range(SLOTS):
            rows = (SLOTS - j) * TOK
            gw = dot(do_own[j * TOK:, :], pair_of(v_all, yy, j), NT)
            dq_acc[j * TOK:, :] += dot((gw * slope[g, j, 0:rows]).astype(BF), pair_of(k_all, yy, j))
        return carry

    def key_back(g):
        yy = near_at(g)
        for j in reversed(range(SLOTS)):
            rows = (j + 1) * TOK
            queries, grads_out = pair_of(q_all, yy, j), pair_of(do_all, yy, j)
            score = dot(k_own[0:rows, :], queries, NT) * SCALE
            gw = dot(v_own[0:rows, :], grads_out, NT)
            place = pair_place(yy, j, lanes)
            begin = start_of(place, [ends[h:h + 1, 0:PAIR] for h in range(3)])
            key_place = place_c[0:rows, :]
            visible = (key_place <= place) & (key_place >= begin)
            gate = jnp.where(visible, jax.nn.sigmoid(score), 0.0)
            weights = score * gate
            dv_acc[0:rows, :] += dot(weights.astype(BF), grads_out)
            dk_acc[0:rows, :] += dot((gw * (gate + weights * (1.0 - gate))).astype(BF), queries)

    remote(ends_own, ends_sib, e_sem.at[0], e_sem.at[1], sibling).start()
    scatter(0, k_ref, k_all.at[block])
    scattered(0)
    scatter(1, v_ref, v_all.at[block])
    for j in range(SLOTS):
        landed(k_all.at[y, j, c], a_recv.at[0, j])
        direct(0, j)
    share(0, 0)
    scattered(1)
    scatter(2, q_ref, q_all.at[block])
    for j in range(SLOTS):
        landed(v_all.at[y, j, c], a_recv.at[1, j])
        direct(1, j)
    share(1, 0)
    att[...] = jnp.zeros_like(att)
    landed(ends_sib, e_sem.at[1])
    ends = jnp.where(row == c, ends_own[...], ends_sib[...])
    for j in range(SLOTS):
        k_own[j * TOK:(j + 1) * TOK, :] = k_all[y, j, c]
        v_own[j * TOK:(j + 1) * TOK, :] = v_all[y, j, c]
        place = (YN * own_z[j] + y) * TOK + lax.broadcasted_iota(jnp.int32, (TOK, 1), 0)
        place_c[j * TOK:(j + 1) * TOK, :] = place
        begin_c[j * TOK:(j + 1) * TOK, :] = start_of(place, [ends[h:h + 1, 0:1] for h in range(3)])
    for j in range(SLOTS):
        forward(0, j)
    share(0, 1)
    share(0, 2)
    scattered(2)
    scatter(3, gh_own, gh_blk.at[slot_of_z])
    for j in range(SLOTS):
        landed(q_all.at[y, j, c], a_recv.at[2, j])
        q_own[j * TOK:(j + 1) * TOK, :] = q_all[y, j, c]

    def forward_step(g, carry):
        @pl.when(g == 0)
        def _():
            shared(0, 0)
            shared(1, 0)

        @pl.when(g == 1)
        def _():
            for j in range(SLOTS):
                forward(1, j)
            share(1, 1)
            share(1, 2)
            share(0, 3)
            for a in range(2):
                shared(a, 1)

        @pl.when(g == 2)
        def _():
            for a in range(2):
                shared(a, 2)

        @pl.when(g == 3)
        def _():
            share(1, 3)
            for j in range(SLOTS):
                direct(2, j)
            share(2, 0)
            for a in range(2):
                shared(a, 3)

        attend(g)
        return carry

    lax.fori_loop(0, 4, forward_step, 0)

    head_cols = pl.ds(pl.multiple_of(head * HEAD, HEAD), HEAD)

    def give_back(src, dst, send, recv, j):
        device, mine = owner[j]

        @pl.when(mine)
        def _():
            pltpu.make_async_copy(src, dst, recv).start()

        @pl.when(jnp.logical_not(mine))
        def _():
            remote(src, dst, send, recv, device).start()

    for j in range(SLOTS):
        landed(gh_blk.at[j], a_recv.at[3, j])
    lane = lax.broadcasted_iota(jnp.int32, (TOK, HEAD), 1)
    for j in range(SLOTS):
        block_gh = gh_blk[j].astype(F32)
        block_att = att[j * TOK:(j + 1) * TOK, :]
        head_mean = jnp.mean(block_att, axis=1, keepdims=True)
        centred = block_att - head_mean
        packed = jnp.where(lane == 0, head_mean, 0.0)
        packed = jnp.where(lane == 1, jnp.sum(centred * centred, axis=1, keepdims=True), packed)
        packed = jnp.where(lane == 2, jnp.sum(block_gh * centred, axis=1, keepdims=True), packed)
        packed = jnp.where(lane == 3, jnp.sum(block_gh, axis=1, keepdims=True), packed)
        stat[head, j] = jnp.transpose(packed)[0:8]
        cen_blk[j] = centred.astype(BF)
    for h in range(HEADS):
        @pl.when(h != head)
        def _():
            remote(stat.at[head], stat.at[head], t_send.at[h], t_recv.at[head],
                   at(c, HEADS * row + h, y)).start()
    for j in range(SLOTS):
        give_back(stat.at[head, j], stat_in.at[head], m_send.at[j], m_recv.at[head], j)
    for j in range(SLOTS):
        give_back(cen_blk.at[j], cen_in.at[:, head_cols], n_send.at[j], n_recv.at[head], j)
    dq_acc[...] = jnp.zeros_like(dq_acc)
    for j in range(SLOTS):
        forward(2, j)

    def combined(parts):
        means = [part[0:1] for part in parts]
        mean = (means[0] + means[1] + means[2] + means[3]) * (1.0 / HEADS)
        square, cross, grad_sum = 0.0, 0.0, 0.0
        for part in parts:
            off = part[0:1] - mean
            square += part[1:2] + HEAD * off * off
            cross += part[2:3] + off * part[3:4]
            grad_sum += part[3:4]
        inv_std = 1.0 / jnp.sqrt(square * (1.0 / QK) + EPS)
        return [mean, inv_std, grad_sum * (1.0 / QK), cross * inv_std * (1.0 / QK)] + means

    def columns(rows):
        pad = jnp.zeros((HEAD - len(rows), TOK), F32)
        cols = jnp.transpose(jnp.concatenate(rows + [pad], axis=0))
        return [cols[:, i:i + 1] for i in range(len(rows))]

    for h in range(HEADS):
        @pl.when(h != head)
        def _():
            landed(stat.at[h], t_recv.at[h])
    for j in reversed(range(SLOTS)):
        mean_c, inv_c, gmean_c, proj_c = columns(combined([stat[h, j] for h in range(HEADS)])[:4])
        unit = (att[j * TOK:(j + 1) * TOK, :] - mean_c) * inv_c
        attn_grad = (inv_c * (gh_blk[j].astype(F32) - gmean_c - unit * proj_c)).astype(BF)
        do_all[y, j, c] = attn_grad
        do_own[j * TOK:(j + 1) * TOK, :] = attn_grad
        direct(3, j)
    share(3, 0)
    share(2, 1)
    share(2, 2)

    def project():
        for h in range(HEADS):
            landed(cen_in.at[:, h * HEAD:(h + 1) * HEAD], n_recv.at[h])
            landed(stat_in.at[h], m_recv.at[h])
        cols = columns(combined([stat_in[h] for h in range(HEADS)]))
        normed = jnp.concatenate([
            cen_in[:, h * HEAD:(h + 1) * HEAD].astype(F32) + (cols[4 + h] - cols[0]) for h in range(HEADS)
        ], axis=1) * cols[1] * gain_ref[...]
        gated = (normed * u_ref[...].astype(F32)).astype(BF)
        w_part[...] = dot(jnp.transpose(gated), og_ref[...]).astype(BF).reshape(4, 2, 64, WIDTH)
        remote(w_part.at[:, 1 - c], w_sib, ws_sem.at[0], ws_sem.at[1], sibling).start()
        norm_own[...] = normed

    def project_out():
        normed = norm_own[...]
        gated = (normed * u_ref[...].astype(F32)).astype(BF)
        gg_out_ref[...] = (gg[...] * normed).astype(BF)
        lay_ref[...] = dot(gated, w_ref[...]).astype(BF)

    HW = WIDTH // 2
    first_half, second_half = pl.ds(0, HW), pl.ds(HW, HW)

    def weight_a():
        landed(w_sib, ws_sem.at[1])
        w_sum[...] = (w_part[:, c].astype(F32) + w_sib[...].astype(F32)).astype(BF).reshape(4, YN, 16, WIDTH)
        for n in range(3):
            to = (x + n + 1) % 4
            remote(w_sum.at[to, :, :, first_half], w_xa.at[n], wx_send.at[n], wx_recv.at[n],
                   (2 * to + c, s)).start()
            to = (y + n + 1) % YN
            remote(w_sum.at[:, to, :, second_half], w_ya.at[n], wy_send.at[n], wy_recv.at[n],
                   at(c, z, to)).start()

    def weight_b():
        for n in range(3):
            landed(w_xa.at[n], wx_recv.at[n])
            landed(w_ya.at[n], wy_recv.at[n])
        w_b[0] = (w_sum[x, :, :, 0:HW].astype(F32) + w_xa[0].astype(F32) + w_xa[1].astype(F32)
                  + w_xa[2].astype(F32)).astype(BF)
        w_b[1] = (w_sum[:, y, :, HW:].astype(F32) + w_ya[0].astype(F32) + w_ya[1].astype(F32)
                  + w_ya[2].astype(F32)).astype(BF)
        for n in range(3):
            to = (y + n + 1) % YN
            remote(w_b.at[0, to], w_yb.at[n], wy_send.at[n + 3], wy_recv.at[n + 3], at(c, z, to)).start()
            to = (x + n + 1) % 4
            remote(w_b.at[1, to], w_xb.at[n], wx_send.at[n + 3], wx_recv.at[n + 3], (2 * to + c, s)).start()

    def weight_z():
        for n in range(3):
            landed(w_yb.at[n], wy_recv.at[n + 3])
            landed(w_xb.at[n], wx_recv.at[n + 3])
        w_16[:, 0:HW] = (w_b[0, y].astype(F32) + w_yb[0].astype(F32) + w_yb[1].astype(F32)
                         + w_yb[2].astype(F32)).astype(BF)
        w_16[:, HW:] = (w_b[1, x].astype(F32) + w_xb[0].astype(F32) + w_xb[1].astype(F32)
                        + w_xb[2].astype(F32)).astype(BF)

        @pl.when(jnp.logical_not(collector))
        def _():
            remote(w_16, w_z.at[z], wz_send, wz_recv.at[z], (d, YN * d + y)).start()

    def weight_all():
        @pl.when(collector)
        def _():
            w_z[z] = w_16[...]
            for zz in range(ZN):
                @pl.when(zz != z)
                def _():
                    landed(w_z.at[zz], wz_recv.at[zz])
            total = w_z[0].astype(F32)
            for zz in range(1, ZN):
                total += w_z[zz].astype(F32)
            w_fin[...] = (total * (ALL_ROWS ** (-0.5))).astype(BF)
            for dd in range(8):
                @pl.when(dd != d)
                def _():
                    remote(w_fin, w_fin, wb_send.at[dd], wb_recv, (dd, s)).start()

    lax.fori_loop(0, 4, attend_back, 0)
    out_blk[2] = (dq_acc[...] * SCALE).astype(BF).reshape(SLOTS, TOK, HEAD)
    for j in range(SLOTS):
        give_back(out_blk.at[2, j], dq_ref.at[:, head_cols], f_send.at[2, j], f_recv.at[2, head], j)
    weight_a()
    dk_acc[...] = jnp.zeros_like(dk_acc)
    dv_acc[...] = jnp.zeros_like(dv_acc)

    def backward_step(g, carry):
        for n in range(4):
            @pl.when(g == n)
            def _():
                if n == 2:
                    share(2, 3)
                    share(3, 3)
                    weight_b()
                for a in (2, 3):
                    shared(a, n)

        key_back(g)
        return carry

    lax.fori_loop(0, 4, backward_step, 0)
    weight_z()
    out_blk[0] = (dk_acc[...] * SCALE).astype(BF).reshape(SLOTS, TOK, HEAD)
    for j in range(SLOTS):
        give_back(out_blk.at[0, j], dk_ref.at[:, head_cols], f_send.at[0, j], f_recv.at[0, head], j)
    out_blk[1] = dv_acc[...].astype(BF).reshape(SLOTS, TOK, HEAD)
    for j in range(SLOTS):
        give_back(out_blk.at[1, j], dv_ref.at[:, head_cols], f_send.at[1, j], f_recv.at[1, head], j)
    project_out()
    weight_all()

    @pl.when(collector)
    def _():
        for dd in range(8):
            @pl.when(dd != d)
            def _():
                sent(w_fin, wb_send.at[dd])

    @pl.when(jnp.logical_not(collector))
    def _():
        landed(w_fin, wb_recv)
        sent(w_16, wz_send)

    wg_ref[...] = w_fin[...].astype(F32)
    for a, dst in ((0, dk_ref), (1, dv_ref), (2, dq_ref)):
        for h in range(HEADS):
            landed(dst.at[:, h * HEAD:(h + 1) * HEAD], f_recv.at[a, h])
    sent(ends_own, e_sem.at[0])
    sent(w_sib, ws_sem.at[0])
    scattered(3)
    for h in range(HEADS):
        @pl.when(h != head)
        def _():
            sent(stat.at[head], t_send.at[h])
    for j in range(SLOTS):
        @pl.when(jnp.logical_not(owner[j][1]))
        def _():
            sent(cen_blk.at[j], n_send.at[j])
            sent(stat_in.at[0], m_send.at[j])
            for a in range(3):
                sent(out_blk.at[a, j], f_send.at[a, j])
        for a in range(4):
            for n in range(2):
                sent(gh_blk.at[0], y_send.at[a, j, n])
                sent(gh_blk.at[0, low], y_send.at[a, j, n + 2])
            sent(k_all.at[0, :, 0], s_send.at[a, j])
    for n in range(3):
        sent(w_xa.at[n], wx_send.at[n])
        sent(w_ya.at[n], wy_send.at[n])
        sent(w_xb.at[n], wx_send.at[n + 3])
        sent(w_yb.at[n], wy_send.at[n + 3])


def copy_kernel(*refs):
    count = len(refs) // 2
    for source, result in zip(refs[:count], refs[count:]):
        result[...] = source[...]


def per_device(queries, keys, values, gates, gain, out_weight, out_grad, lengths):
    vm = pl.BlockSpec(memory_space=pltpu.VMEM)
    anywhere = pl.BlockSpec(memory_space=pl.ANY)
    block = (SLOTS, TOK, HEAD)
    whole = (YN, SLOTS, 2, TOK, HEAD)
    own = (CHUNK, HEAD)
    dma = pltpu.SemaphoreType.DMA
    scratch = [
        pltpu.VMEM(whole, BF),
        pltpu.VMEM(whole, BF),
        pltpu.VMEM(whole, BF),
        pltpu.VMEM(whole, BF),
        pltpu.VMEM((TOK, QK), BF),
        pltpu.VMEM((TOK, WIDTH), BF),
        pltpu.VMEM((QK, WIDTH), BF),
        pltpu.VMEM(block, BF),
        pltpu.VMEM((TOK, QK), BF),
        pltpu.VMEM((TOK, QK), F32),
        pltpu.VMEM((8, CHUNK), jnp.int32),
        pltpu.VMEM((8, CHUNK), jnp.int32),
        pltpu.VMEM(own, F32),
        pltpu.VMEM((YN, SLOTS, CHUNK, PAIR), F32),
        pltpu.VMEM(own, BF),
        pltpu.VMEM(own, BF),
        pltpu.VMEM(own, BF),
        pltpu.VMEM(own, BF),
        pltpu.VMEM((CHUNK, 1), jnp.int32),
        pltpu.VMEM((CHUNK, 1), jnp.int32),
        pltpu.VMEM((HEADS, SLOTS, 8, TOK), F32),
        pltpu.VMEM((HEADS, 8, TOK), F32),
        pltpu.VMEM(block, BF),
        pltpu.VMEM((TOK, QK), BF),
        pltpu.VMEM((TOK, QK), F32),
        pltpu.VMEM(own, F32),
        pltpu.VMEM(own, F32),
        pltpu.VMEM(own, F32),
        pltpu.VMEM((3, SLOTS, TOK, HEAD), BF),
        pltpu.VMEM((4, 2, 64, WIDTH), BF),
        pltpu.VMEM((4, 64, WIDTH), BF),
        pltpu.VMEM((4, YN, 16, WIDTH), BF),
        pltpu.VMEM((3, YN, 16, WIDTH // 2), BF),
        pltpu.VMEM((3, YN, 16, WIDTH // 2), BF),
        pltpu.VMEM((2, YN, 16, WIDTH // 2), BF),
        pltpu.VMEM((3, 16, WIDTH // 2), BF),
        pltpu.VMEM((3, 16, WIDTH // 2), BF),
        pltpu.VMEM((16, WIDTH), BF),
        pltpu.VMEM((ZN, 16, WIDTH), BF),
        pltpu.VMEM((16, WIDTH), BF),
        dma((3,)),
        dma((4, 4)), dma((4, 4)),
        dma((4, 4, 4)), dma((4, 4, 4)),
        dma((4, 4)), dma((4, 4)),
        dma((2,)),
        dma((4,)), dma((4,)),
        dma((4,)), dma((4,)),
        dma((4,)), dma((4,)),
        dma((3, 4)), dma((3, 4)),
        dma((2,)),
        dma((6,)), dma((6,)),
        dma((6,)), dma((6,)),
        dma, dma((8,)),
        dma((8,)), dma,
    ]
    shapes = (
        jax.ShapeDtypeStruct((TOK, WIDTH), BF),
        jax.ShapeDtypeStruct((TOK, QK), BF),
        jax.ShapeDtypeStruct((TOK, QK), BF),
        jax.ShapeDtypeStruct((TOK, QK), BF),
        jax.ShapeDtypeStruct((TOK, QK), BF),
        jax.ShapeDtypeStruct((16, WIDTH), F32),
    )
    results = pl.pallas_call(
        layer_kernel,
        out_shape=shapes,
        in_specs=[anywhere] * 6 + [vm] * 2,
        out_specs=(vm,) * 6,
        scratch_shapes=scratch,
        compiler_params=pltpu.CompilerParams(
            collective_id=0, has_side_effects=True, vmem_limit_bytes=56 * 1024 * 1024
        ),
    )(
        queries, keys, values, gates, out_grad, out_weight,
        gain.reshape(1, QK), lengths,
    )
    return pl.pallas_call(
        copy_kernel,
        out_shape=shapes,
        in_specs=[vm] * 6,
        out_specs=(vm,) * 6,
    )(*results)


def solution(mesh):
    rows = P(("dp", "seq"), None)

    def program(queries, keys, values, gates, gain, out_weight, out_grad, lengths):
        return jax.shard_map(
            per_device,
            mesh=mesh,
            in_specs=(rows, rows, rows, rows, P(), P(), rows, P("dp", None)),
            out_specs=(rows, rows, rows, rows, rows, P("seq", None)),
            check_vma=False,
        )(queries, keys, values, gates, gain, out_weight, out_grad, lengths)

    return program
```
